128 devices in a mesh: ctx: 32 (over z, x, core), head: 4 (over y).
Axes of the slice: x: 4, y: 4, z: 4, core: 2. Of those that a mesh axis runs over, the one named last changes fastest.
Arguments:
- queries: bfloat16 [384, 5120], P('ctx', 'head'), as said below
- draft_keys: bfloat16 [384, 1024], P('ctx', 'head'), may hold values from -2.5 to 2.5
- draft_values: bfloat16 [384, 1024], P('ctx', 'head'), may hold values from -6 to 6
- cache_keys: bfloat16 [2048, 128, 8, 128], P('ctx', None, 'head'), as said below
- cache_values: bfloat16 [2048, 128, 8, 128], P('ctx', None, 'head'), may hold values from -6 to 6
- w_out: bfloat16 [5120, 5120], P('head', 'ctx'), may hold values from -0.078125 to 0.078125
- lengths: int32 [24], replicated, may hold values from 1 to 65536, as said below
- block_req: int32 [2048], replicated, may hold values from 0 to 23, as said below
- block_idx: int32 [2048], replicated, may hold values from -1 to 511
- move_dst: int32 [2048], replicated, may hold values from -1 to 31, as said below
- draft_offs: int32 [24, 16], replicated, may hold values from 0 to 15, as said below
Outputs:
- mixed: bfloat16 [384, 5120], P('head', 'ctx')
- new_keys: bfloat16 [3072, 128, 8, 128], P('ctx', None, 'head')
- new_values: bfloat16 [3072, 128, 8, 128], P('ctx', None, 'head')
The draws below stay inside these ranges and needn't reach their ends.
Inputs may be any that keep to these rules, and one draw needn't show every extreme that they name: queries lie within -6 to 6. cache_keys lie within -6 to 6. Request r has exactly ceil(lengths[r] / 128) blocks, numbered from 0, each in exactly one slot. Empty slots hold block_req 0; on each index of ctx the live slots come before the empty ones. `move_dst`: only live blocks move, never to their own index; at most 2 blocks go from one index of ctx to one other and at most 32 arrive at one index, both reached. draft_offs[r, t] <= t.
All inputs are finite; a program needn't handle non-finite values.
Results may differ from the reference program's by a relative error of at most 0.0051.
Values may be sent and summed in bfloat16 or wider, within the bound.
No kernel may reach another device: no remote copies, remote signals or barrier semaphores. Data moves between devices by JAX's collectives and lax.ppermute only.
A program may use at most 128 MiB of HBM per device.

```python
import math
import jax
import jax.numpy as jnp
from jax import lax

D = 5120
QH = 40
KVH = 8
HD = 128
GROUP = 5
DRAFT = 16
REQS = 24
BLK = 128
BLOCKS_DEV = 64
IN_DEV = 32
NBLK = 2048
TOKENS = 384
N_CTX = 32


def draw_queries(key, part):
    values = jax.random.uniform(key, (TOKENS, QH * HD), jnp.float32, -6.0, 6.0)
    return values.astype(jnp.bfloat16)


def draw_cache_keys(key, part):
    values = jnp.clip(0.3 * jax.random.normal(key, (NBLK, BLK, KVH, HD), jnp.float32), -6.0, 6.0)
    return values.astype(jnp.bfloat16)


def plan_tables(key):
    base = jax.random.fold_in(key, 9173)
    keys = jax.random.split(base, 6)
    ndev = NBLK // BLOCKS_DEV
    half = ndev // 2
    devs = jnp.arange(ndev, dtype=jnp.int32)
    shuffled = jax.random.permutation(keys[0], ndev - 1).astype(jnp.int32)
    rank_of = jnp.full((ndev,), ndev - 1, jnp.int32).at[shuffled].set(jnp.arange(ndev - 1, dtype=jnp.int32))
    heavy = (rank_of < half).astype(jnp.int32)
    light = 1 - heavy
    receiver = jnp.sum(jnp.where(rank_of == half, devs, 0))
    low = jax.random.randint(keys[1], (ndev,), BLOCKS_DEV // 4, BLOCKS_DEV // 2 + 1).astype(jnp.int32)
    count = jnp.where(heavy == 1, BLOCKS_DEV, low).astype(jnp.int32)
    moves = jax.random.randint(keys[2], (ndev, ndev), 1, 3).astype(jnp.int32) * heavy[:, None] * light[None, :]
    moves = jnp.where((devs[None, :] == receiver) & (heavy[:, None] == 1), 2, moves).astype(jnp.int32)
    out_count = jnp.sum(moves, axis=1)
    cum = jnp.cumsum(moves, axis=1)
    slots = jnp.arange(BLOCKS_DEV, dtype=jnp.int32)
    offset = slots[None, :] - (count - out_count)[:, None]
    live = slots[None, :] < count[:, None]
    moved = (offset >= 0) & live
    dst = jnp.sum((cum[:, None, :] <= offset[:, :, None]).astype(jnp.int32), axis=2)
    move_dst = jnp.where(moved, dst, -1).astype(jnp.int32).reshape(-1)
    start_dev = jnp.cumsum(count) - count
    rank = start_dev[:, None] + slots[None, :]
    total = jnp.sum(count)
    longest = NBLK // 4
    reqs_line = jnp.arange(REQS, dtype=jnp.int32)
    long_id = jax.random.randint(keys[5], (), 0, REQS).astype(jnp.int32)
    is_long = reqs_line == long_id
    weights = jnp.where(is_long, 0, 1 + jax.random.randint(keys[3], (REQS,), 0, 2)).astype(jnp.int32)
    extra = total - longest - (REQS - 1)
    cum_in = jnp.cumsum(weights)
    cum_ex = cum_in - weights
    wsum = jnp.sum(weights)
    others = 1 + extra * cum_in // wsum - extra * cum_ex // wsum
    blocks_of = jnp.where(is_long, longest, others).astype(jnp.int32)
    start = jnp.cumsum(blocks_of) - blocks_of
    req = jnp.sum((start[None, None, :] <= rank[:, :, None]).astype(jnp.int32), axis=2) - 1
    req = jnp.clip(req, 0, REQS - 1)
    idx = rank - jnp.take(start, req)
    block_req = jnp.where(live, req, 0).astype(jnp.int32).reshape(-1)
    block_idx = jnp.where(live, idx, -1).astype(jnp.int32).reshape(-1)
    trim = jnp.where(is_long, 0, jax.random.randint(keys[4], (REQS,), 0, BLK - 1))
    lengths = (blocks_of * BLK - trim).astype(jnp.int32)
    return (lengths, block_req, block_idx, move_dst)


def draw_lengths(key, part):
    return plan_tables(key)[0]


def draw_block_req(key, part):
    return plan_tables(key)[1]


def draw_block_idx(key, part):
    return plan_tables(key)[2]


def draw_move_dst(key, part):
    return plan_tables(key)[3]


def draw_draft_offs(key, part):
    base = jax.random.fold_in(key, 3307)
    tpos = jnp.arange(DRAFT, dtype=jnp.int32)
    offs = jax.random.randint(base, (REQS, DRAFT), 0, tpos[None, :] + 1).astype(jnp.int32)
    return offs.at[0, DRAFT - 1].set(DRAFT - 1)


def block_levels(stream_key, shape, cuts, low, high):
    def one(position, parts):
        steps = jax.random.uniform(jax.random.fold_in(jax.random.fold_in(stream_key, 6), position), (parts,), jnp.float32, low / len(cuts), high / len(cuts))
        return jnp.repeat(jnp.exp(steps), shape[position] // parts).reshape((-1,) + (1,) * (len(shape) - position - 1))

    level = one(*cuts[0])
    for cut in cuts[1:]:
        level = level * one(*cut)
    return level


def gaussian(key, dims, scale, limit, shards=(), held_as=jnp.bfloat16):
    result = jax.random.normal(key, dims, jnp.float32) * scale
    if len(shards) > 0:
        result = block_levels(key, dims, shards, -0.22, 0.18) * result
    return jnp.clip(result, min=-limit, max=limit).astype(held_as)


def setup_inputs(seed: int = 0) -> dict:
    arg_keys = jax.random.split(jax.random.key(seed), 12)
    return {
        "queries": draw_queries(jax.random.fold_in(arg_keys[11], 71), 0),
        "draft_keys": gaussian(arg_keys[1], (TOKENS, KVH * HD), 0.3, 2.5, ((0, 32), (1, 4))),
        "draft_values": gaussian(arg_keys[2], (TOKENS, KVH * HD), 1.0, 6.0, ((0, 32), (1, 4))),
        "cache_keys": draw_cache_keys(jax.random.fold_in(arg_keys[11], 71), 0),
        "cache_values": gaussian(arg_keys[4], (NBLK, BLK, KVH, HD), 1.0, 6.0, ((0, 32), (2, 4))),
        "w_out": gaussian(arg_keys[5], (QH * HD, D), (QH * HD) ** -0.5, 0.078125, ((0, 4), (1, 32))),
        "lengths": draw_lengths(jax.random.fold_in(arg_keys[11], 71), 0),
        "block_req": draw_block_req(jax.random.fold_in(arg_keys[11], 71), 0),
        "block_idx": draw_block_idx(jax.random.fold_in(arg_keys[11], 71), 0),
        "move_dst": draw_move_dst(jax.random.fold_in(arg_keys[11], 71), 0),
        "draft_offs": draw_draft_offs(jax.random.fold_in(arg_keys[11], 71), 0),
    }


def live_tokens(lengths, block_req, block_idx):
    own_len = jnp.take(lengths, block_req) - block_idx * BLK
    counts = jnp.where(block_idx >= 0, jnp.clip(own_len, 0, BLK), 0)
    return jnp.arange(BLK, dtype=jnp.int32)[None, :] < counts[:, None]

def draft_seen(draft_offs):
    tpos = jnp.arange(DRAFT, dtype=jnp.int32)
    return (tpos[None, None, :] >= draft_offs[:, :, None]) & (tpos[None, None, :] <= tpos[None, :, None])

def relocate(cache, move_dst):
    every = jnp.arange(NBLK, dtype=jnp.int32)
    moved = move_dst >= 0
    earlier = (move_dst[:, None] == move_dst[None, :]) & (every[None, :] < every[:, None])
    order = lax.optimization_barrier(jnp.sum(earlier.astype(jnp.int32), axis=1))
    width = BLOCKS_DEV + IN_DEV
    home = every // BLOCKS_DEV * width + every % BLOCKS_DEV
    away = jnp.where(moved, move_dst * width + BLOCKS_DEV + order, N_CTX * width)
    kept = jnp.where(moved[:, None, None, None], jnp.zeros_like(cache), cache)
    fresh = jnp.zeros((N_CTX * width,) + cache.shape[1:], cache.dtype)
    fresh = fresh.at[home].set(kept)
    return fresh.at[away].set(cache, mode='drop')

def reference(queries, draft_keys, draft_values, cache_keys, cache_values, w_out, lengths, block_req, block_idx, move_dst, draft_offs):
    scale = 1.0 / math.sqrt(HD)
    live = live_tokens(lengths, block_req, block_idx)
    seen = draft_seen(draft_offs)
    onehot = block_req[None, :] == jnp.arange(REQS, dtype=jnp.int32)[:, None]
    onehot_f = onehot.astype(jnp.float32)
    q_heads = jnp.transpose(queries.reshape(REQS, DRAFT, KVH, GROUP, HD), (2, 0, 1, 3, 4))
    k_heads = jnp.transpose(cache_keys, (2, 0, 1, 3))
    v_heads = jnp.transpose(cache_values, (2, 0, 1, 3))
    dk_heads = jnp.transpose(draft_keys.reshape(REQS, DRAFT, KVH, HD), (2, 0, 1, 3))
    dv_heads = jnp.transpose(draft_values.reshape(REQS, DRAFT, KVH, HD), (2, 0, 1, 3))

    def one_head(items):
        q_one, k_one, v_one, dk_one, dv_one = items
        q_slot = jnp.take(q_one, block_req, axis=0)
        scores = jnp.einsum('btgd,bjd->btgj', q_slot.astype(jnp.float32), k_one.astype(jnp.float32)) * scale
        scores = jnp.where(live[:, None, None, :], scores, -jnp.inf)
        block_top = lax.optimization_barrier(jnp.max(scores, axis=3))
        cache_top = lax.optimization_barrier(jnp.max(jnp.where(onehot[:, :, None, None], block_top[None], -jnp.inf), axis=1))
        dscores = jnp.einsum('rtgd,rud->rtgu', q_one.astype(jnp.float32), dk_one.astype(jnp.float32)) * scale
        dscores = jnp.where(seen[:, :, None, :], dscores, -jnp.inf)
        top = jnp.maximum(cache_top, lax.optimization_barrier(jnp.max(dscores, axis=3)))
        probs = jnp.where(live[:, None, None, :], jnp.exp(scores - jnp.take(top, block_req, axis=0)[..., None]), 0.0)
        dprobs = jnp.where(seen[:, :, None, :], jnp.exp(dscores - top[..., None]), 0.0)
        denom = jnp.einsum('rb,btg->rtg', onehot_f, lax.optimization_barrier(jnp.sum(probs, axis=3)), precision=lax.Precision.HIGHEST) + lax.optimization_barrier(jnp.sum(dprobs, axis=3))
        pbf = probs.astype(jnp.bfloat16).astype(jnp.float32)
        slot_numer = jnp.einsum('btgj,bjd->btgd', pbf, v_one.astype(jnp.float32))
        numer = jnp.einsum('rb,btgd->rtgd', onehot_f, slot_numer, precision=lax.Precision.HIGHEST)
        dpbf = dprobs.astype(jnp.bfloat16).astype(jnp.float32)
        numer = numer + jnp.einsum('rtgu,rud->rtgd', dpbf, dv_one.astype(jnp.float32))
        return (numer / denom[..., None]).astype(jnp.bfloat16)
    heads_out = lax.map(one_head, (q_heads, k_heads, v_heads, dk_heads, dv_heads))
    attn = jnp.transpose(heads_out, (1, 2, 0, 3, 4)).reshape(TOKENS, QH * HD)
    mixed = jnp.dot(attn, w_out, preferred_element_type=jnp.float32).astype(jnp.bfloat16)
    return (mixed, relocate(cache_keys, move_dst), relocate(cache_values, move_dst))
```

```python
import functools
import math

import jax
import jax.numpy as jnp
from jax import lax
from jax.experimental import pallas as pl
from jax.experimental.pallas import tpu as pltpu
from jax.sharding import PartitionSpec as P

CAP = 2
STEP = 4
LOW = -1e30


def pack_kernel(rank_ref, dst_ref, k_ref, v_ref, send_ref, used, sems):
    blocks = k_ref.shape[0]
    base = rank_ref[0] * blocks

    def clear(d, carry):
        used[d] = 0
        return carry

    lax.fori_loop(0, used.shape[0], clear, 0)

    def copies(b, row):
        return (
            pltpu.make_async_copy(k_ref.at[b], send_ref.at[row, 0], sems.at[b, 0]),
            pltpu.make_async_copy(v_ref.at[b], send_ref.at[row, 1], sems.at[b, 1]),
        )

    def start(b, carry):
        dst = dst_ref[base + b]

        @pl.when(dst >= 0)
        def _():
            place = used[dst]
            used[dst] = place + 1
            for c in copies(b, dst * CAP + place):
                c.start()

        return carry

    lax.fori_loop(0, blocks, start, 0)

    def finish(b, carry):
        @pl.when(dst_ref[base + b] >= 0)
        def _():
            for c in copies(b, 0):
                c.wait()

        return carry

    lax.fori_loop(0, blocks, finish, 0)


def pack(rank, move_dst, keys, values, nctx):
    blocks, rows, lanes = keys.shape
    return pl.pallas_call(
        pack_kernel,
        out_shape=jax.ShapeDtypeStruct((nctx * CAP, 2, rows, lanes), keys.dtype),
        grid_spec=pltpu.PrefetchScalarGridSpec(
            num_scalar_prefetch=2,
            grid=(1,),
            in_specs=[pl.BlockSpec(memory_space=pl.ANY)] * 2,
            out_specs=pl.BlockSpec(memory_space=pl.ANY),
            scratch_shapes=[
                pltpu.SMEM((nctx,), jnp.int32),
                pltpu.SemaphoreType.DMA((blocks, 2)),
            ],
        ),
        cost_estimate=pl.CostEstimate(
            flops=0, bytes_accessed=4 * blocks * rows * lanes * 2, transcendentals=0
        ),
        name="pack",
    )(rank, move_dst, keys, values)


def unpack_kernel(count_ref, recv_ref, k_in, v_in, k_out, v_out, zero, sems):
    del k_in, v_in
    nctx = count_ref.shape[0]
    slots = sems.shape[0]
    first = k_out.shape[0] - slots
    zero[...] = jnp.zeros_like(zero)

    def copies(row, slot):
        return (
            pltpu.make_async_copy(recv_ref.at[row, 0], k_out.at[first + slot], sems.at[slot, 0]),
            pltpu.make_async_copy(recv_ref.at[row, 1], v_out.at[first + slot], sems.at[slot, 1]),
        )

    def blanks(slot):
        return (
            pltpu.make_async_copy(zero, k_out.at[first + slot], sems.at[slot, 0]),
            pltpu.make_async_copy(zero, v_out.at[first + slot], sems.at[slot, 1]),
        )

    def source(s, slot):
        count = count_ref[s]
        for place in range(CAP):

            @pl.when((count > place) & (slot + place < slots))
            def _():
                for c in copies(s * CAP + place, slot + place):
                    c.start()

        return slot + count

    filled = jnp.minimum(lax.fori_loop(0, nctx, source, 0), slots)

    def blank(slot, carry):
        for c in blanks(slot):
            c.start()
        return carry

    lax.fori_loop(filled, slots, blank, 0)

    def finish(slot, carry):
        for c in copies(0, slot):
            c.wait()
        return carry

    lax.fori_loop(0, slots, finish, 0)


def unpack(count, recv, keys, values, slots):
    rows, lanes = keys.shape[1:]
    shape = jax.ShapeDtypeStruct(keys.shape, keys.dtype)
    return pl.pallas_call(
        unpack_kernel,
        out_shape=(shape, shape),
        grid_spec=pltpu.PrefetchScalarGridSpec(
            num_scalar_prefetch=1,
            grid=(1,),
            in_specs=[pl.BlockSpec(memory_space=pl.ANY)] * 3,
            out_specs=[pl.BlockSpec(memory_space=pl.ANY)] * 2,
            scratch_shapes=[
                pltpu.VMEM((rows, lanes), keys.dtype),
                pltpu.SemaphoreType.DMA((slots, 2)),
            ],
        ),
        input_output_aliases={2: 0, 3: 1},
        cost_estimate=pl.CostEstimate(
            flops=0, bytes_accessed=8 * slots * rows * lanes, transcendentals=0
        ),
        name="unpack",
    )(count, recv, keys, values)


def attend(q, keys, values, column, limit, top, total, numer, r, log_scale):
    scores = lax.dot_general(q, keys, (((1,), (1,)), ((), ())), preferred_element_type=jnp.float32)
    scores = jnp.where(column < limit, scores, LOW)
    best = jnp.max(scores, axis=1, keepdims=True)
    best = best.astype(jnp.bfloat16).astype(jnp.float32)
    old = top[r]
    new = jnp.maximum(old, best)
    probs = jnp.exp2((scores - new[:, :1]) * log_scale)
    shrink = jnp.exp2((old - new) * log_scale)
    top[r] = new
    lanes = numer.shape[2]
    width = probs.shape[1]
    if width > lanes:
        part = probs[:, :lanes]
        for first in range(lanes, width, lanes):
            part = part + probs[:, first : first + lanes]
    else:
        part = jnp.concatenate(
            [probs, jnp.zeros((probs.shape[0], lanes - width), jnp.float32)], axis=1
        )
    total[r] = total[r] * shrink + part
    numer[r] = numer[r] * shrink + jnp.dot(
        probs.astype(jnp.bfloat16), values, preferred_element_type=jnp.float32
    )


def attention_kernel(
    kv_local, group, log_scale,
    rank_ref, req_ref, idx_ref, dst_ref, len_ref,
    q_ref, dk_ref, dv_ref, offs_ref, k_ref, v_ref,
    numer_ref, stats_ref, k_out, v_out,
    top, total, numer, column,
):
    step = pl.program_id(0)
    requests, rows, lanes = numer.shape
    width = k_ref.shape[1] // kv_local
    blocks = pl.num_programs(0) * STEP
    rank = rank_ref[0]
    base = rank * blocks + step * STEP

    @pl.when(step == 0)
    def _():
        top[...] = jnp.full(top.shape, LOW, jnp.float32)
        total[...] = jnp.zeros(total.shape, jnp.float32)
        numer[...] = jnp.zeros(numer.shape, jnp.float32)
        line = lax.broadcasted_iota(jnp.int32, column.shape, 1)
        row = lax.broadcasted_iota(jnp.int32, column.shape, 0)
        own = row % (kv_local * group) // group
        column[...] = jnp.where(line % kv_local == own, line // kv_local, 1 << 20)

        @pl.when(rank < requests)
        def _():
            drafts = dk_ref.shape[1]
            spot = column[:, :drafts]
            spot = jnp.where(spot >= offs_ref[...], spot, 1 << 20)
            token = lax.broadcasted_iota(jnp.int32, spot.shape, 0) // (kv_local * group)
            attend(q_ref[rank], dk_ref[rank], dv_ref[rank], spot, token + 1,
                   top, total, numer, rank, log_scale)

    for g in range(STEP):
        slot = base + g
        stays = dst_ref[slot] < 0

        @pl.when(stays)
        def _():
            k_out[g] = k_ref[g]
            v_out[g] = v_ref[g]

        @pl.when(jnp.logical_not(stays))
        def _():
            k_out[g] = jnp.zeros(k_out.shape[1:], k_out.dtype)
            v_out[g] = jnp.zeros(v_out.shape[1:], v_out.dtype)

        idx = idx_ref[slot]

        @pl.when(idx >= 0)
        def _():
            r = req_ref[slot]
            limit = jnp.minimum(len_ref[r] - idx * width, width)
            attend(q_ref[r], k_ref[g], v_ref[g], column[...], limit,
                   top, total, numer, r, log_scale)

    @pl.when(step == pl.num_programs(0) - 1)
    def _():
        ones = jnp.ones((8, lanes), jnp.float32)
        first = (lax.broadcasted_iota(jnp.int32, (8, lanes), 1) == 0).astype(jnp.float32)
        pick = lax.broadcasted_iota(jnp.int32, (8, rows), 0)
        turn = (((1,), (1,)), ((), ()))

        def close(r, carry):
            numer_ref[r] = numer[r].astype(numer_ref.dtype)
            sums = lax.dot_general(ones, total[r], turn, precision=lax.Precision.HIGHEST,
                                   preferred_element_type=jnp.float32)
            tops = lax.dot_general(first, top[r], turn, precision=lax.Precision.HIGHEST,
                                   preferred_element_type=jnp.float32)
            stats_ref[r] = jnp.where(pick == 0, tops, sums)
            return carry

        lax.fori_loop(0, requests, close, 0)


def attention(rank, block_req, block_idx, move_dst, lengths, q, dk, dv, offs, keys, values,
              slots, kv_local, group, log_scale):
    blocks, width, lanes = keys.shape
    requests, rows, _ = q.shape
    whole = lambda shape: pl.BlockSpec(shape, lambda i, *_: (0,) * len(shape))
    part = pl.BlockSpec((STEP, width, lanes), lambda i, *_: (i, 0, 0))
    cache = jax.ShapeDtypeStruct((blocks + slots, width, lanes), keys.dtype)
    return pl.pallas_call(
        functools.partial(attention_kernel, kv_local, group, log_scale),
        out_shape=(
            jax.ShapeDtypeStruct((requests, rows, lanes), jnp.bfloat16),
            jax.ShapeDtypeStruct((requests, 8, rows), jnp.float32),
            cache,
            cache,
        ),
        grid_spec=pltpu.PrefetchScalarGridSpec(
            num_scalar_prefetch=5,
            grid=(blocks // STEP,),
            in_specs=[whole(q.shape), whole(dk.shape), whole(dv.shape), whole(offs.shape), part, part],
            out_specs=[whole((requests, rows, lanes)), whole((requests, 8, rows)), part, part],
            scratch_shapes=[
                pltpu.VMEM((requests, rows, lanes), jnp.float32),
                pltpu.VMEM((requests, rows, lanes), jnp.float32),
                pltpu.VMEM((requests, rows, lanes), jnp.float32),
                pltpu.VMEM((rows, width), jnp.int32),
            ],
        ),
        compiler_params=pltpu.CompilerParams(vmem_limit_bytes=40 * 2**20),
        cost_estimate=pl.CostEstimate(
            flops=4 * blocks * rows * width * lanes,
            bytes_accessed=8 * blocks * width * lanes,
            transcendentals=blocks * rows * width,
        ),
        name="attention",
    )(rank, block_req, block_idx, move_dst, lengths, q, dk, dv, offs, keys, values)


def exchange(x, axis):
    return lax.all_to_all(x, axis, split_axis=0, concat_axis=0, tiled=True)


def everywhere(x, axis):
    n = lax.axis_size(axis)
    return exchange(jnp.broadcast_to(x[None], (n, *x.shape)), axis)


def shards(
    queries, draft_keys, draft_values, cache_keys, cache_values, w_out,
    lengths, block_req, block_idx, move_dst, draft_offs,
):
    blocks, width, kv_local, head_dim = cache_keys.shape
    nctx = lax.axis_size("ctx")
    rank = lax.axis_index("ctx").astype(jnp.int32)
    requests, drafts = draft_offs.shape
    own = queries.shape[0]
    heads = queries.shape[1] // head_dim
    group = heads // kv_local
    tokens = requests * drafts
    slots = nctx
    log_scale = math.log2(math.e) / math.sqrt(head_dim)
    me = rank.reshape(1)

    keys = cache_keys.reshape(blocks, width * kv_local, head_dim)
    values = cache_values.reshape(blocks, width * kv_local, head_dim)

    mine = jnp.concatenate(
        [
            queries.reshape(own * heads, head_dim),
            draft_keys.reshape(own * kv_local, head_dim),
            draft_values.reshape(own * kv_local, head_dim),
        ],
        axis=0,
    )
    shared = everywhere(mine, "ctx")
    cut = own * heads
    cut2 = cut + own * kv_local
    q = shared[:, :cut].reshape(requests, drafts * heads, head_dim)
    dk = shared[:, cut:cut2].reshape(requests, drafts * kv_local, head_dim)
    dv = shared[:, cut2:].reshape(requests, drafts * kv_local, head_dim)

    send = pack(me, move_dst, keys, values, nctx)
    recv = exchange(send, "ctx")

    my_offs = lax.dynamic_slice_in_dim(draft_offs, jnp.minimum(rank, requests - 1), 1)[0]
    offs = jnp.repeat(my_offs, heads)[:, None]
    numer, stats, new_keys, new_values = attention(
        me, block_req, block_idx, move_dst, lengths, q, dk, dv, offs, keys, values,
        slots, kv_local, group, log_scale,
    )
    rows = own * heads
    tops = stats[:, 0].reshape(nctx, 1, rows)
    sums = stats[:, 1].reshape(nctx, 1, rows)
    high = sums.astype(jnp.bfloat16)
    rest = (sums - high.astype(jnp.float32)).astype(jnp.bfloat16)
    notes = jnp.concatenate([tops.astype(jnp.bfloat16), high, rest], axis=1)
    notes = jnp.pad(notes, ((0, 0), (0, 5), (0, head_dim - rows)))
    parts = exchange(
        jnp.concatenate([numer.reshape(nctx, rows, head_dim), notes], axis=1), "ctx"
    )
    notes = parts[:, rows : rows + 3, :rows].astype(jnp.float32)
    top = jnp.max(notes[:, 0], axis=0)
    factor = jnp.exp2((notes[:, 0] - top) * log_scale)
    denom = jnp.sum(factor * (notes[:, 1] + notes[:, 2]), axis=0)
    total = jnp.sum(parts[:, :rows].astype(jnp.float32) * factor[:, :, None], axis=0)
    attn = (total / denom[:, None]).astype(jnp.bfloat16)
    attn = everywhere(attn.reshape(own, heads * head_dim), "ctx").reshape(tokens, heads * head_dim)
    partial = jnp.dot(attn, w_out, preferred_element_type=jnp.float32)
    nhead = lax.axis_size("head")
    mixed = jnp.sum(
        exchange(partial.reshape(nhead, tokens // nhead, -1), "head"), axis=0
    ).astype(jnp.bfloat16)

    count = jnp.sum((move_dst.reshape(nctx, blocks) == rank).astype(jnp.int32), axis=1)
    new_keys, new_values = unpack(count, recv, new_keys, new_values, slots)
    shape = (blocks + slots, width, kv_local, head_dim)
    return (mixed, new_keys.reshape(shape), new_values.reshape(shape))


def solution(mesh):
    cache = P("ctx", None, "head", None)
    in_specs = (
        P("ctx", "head"), P("ctx", "head"), P("ctx", "head"), cache, cache, P("head", "ctx"),
        P(), P(), P(), P(), P(),
    )
    out_specs = (P("head", "ctx"), cache, cache)
    return jax.shard_map(shards, mesh=mesh, in_specs=in_specs, out_specs=out_specs, check_vma=False)
```

```python
import functools
import math

import jax
import jax.numpy as jnp
from jax import lax
from jax.experimental import pallas as pl
from jax.experimental.pallas import tpu as pltpu
from jax.sharding import PartitionSpec as P

CAP = 2
STEP = 4
LOW = -1e30


def pack_kernel(rank_ref, dst_ref, k_ref, v_ref, first_ref, second_ref, third_ref, used, sems):
    blocks, rows, _ = k_ref.shape
    lead = second_ref.shape[1] - rows
    base = rank_ref[0] * blocks

    def clear(d, carry):
        used[d] = 0
        return carry

    lax.fori_loop(0, used.shape[0], clear, 0)

    def start(b, carry):
        dst = dst_ref[base + b]

        @pl.when(dst >= 0)
        def _():
            place = used[dst]
            used[dst] = place + 1
            pltpu.make_async_copy(k_ref.at[b], first_ref.at[dst, place], sems.at[b, 0]).start()
            for p, out in enumerate((second_ref, third_ref)):

                @pl.when(place == p)
                def _():
                    pltpu.make_async_copy(
                        v_ref.at[b], out.at[dst, pl.ds(lead, rows)], sems.at[b, 1]
                    ).start()

        return carry

    lax.fori_loop(0, blocks, start, 0)

    def finish(b, carry):
        @pl.when(dst_ref[base + b] >= 0)
        def _():
            for i in range(2):
                pltpu.make_async_copy(k_ref.at[b], first_ref.at[0, 0], sems.at[b, i]).wait()

        return carry

    lax.fori_loop(0, blocks, finish, 0)


def pack(rank, move_dst, keys, values, nctx, lead):
    blocks, rows, lanes = keys.shape
    later = jax.ShapeDtypeStruct((nctx, lead + rows, lanes), keys.dtype)
    return pl.pallas_call(
        pack_kernel,
        out_shape=(jax.ShapeDtypeStruct((nctx, CAP, rows, lanes), keys.dtype), later, later),
        grid_spec=pltpu.PrefetchScalarGridSpec(
            num_scalar_prefetch=2,
            grid=(1,),
            in_specs=[pl.BlockSpec((blocks, rows, lanes), lambda i, *_: (0, 0, 0))] * 2,
            out_specs=[pl.BlockSpec(memory_space=pl.ANY)] * 3,
            scratch_shapes=[
                pltpu.SMEM((nctx,), jnp.int32),
                pltpu.SemaphoreType.DMA((blocks, 2)),
            ],
        ),
        compiler_params=pltpu.CompilerParams(vmem_limit_bytes=40 * 2**20),
        cost_estimate=pl.CostEstimate(
            flops=0, bytes_accessed=4 * blocks * rows * lanes * 2, transcendentals=0
        ),
        name="pack",
    )(rank, move_dst, keys, values)


def unpack_kernel(places, slots, count_ref, *refs):
    recvs, (_, out_ref, stage, loads, stores) = refs[:-5], refs[-5:]
    nctx = count_ref.shape[0]
    rows = out_ref.shape[1]
    first = out_ref.shape[0] - slots

    def load(which, lead, source, slot):
        return pltpu.make_async_copy(
            recvs[which].at[source, pl.ds(lead, rows)], stage.at[slot], loads.at[slot]
        )

    def store(slot):
        return pltpu.make_async_copy(stage.at[slot], out_ref.at[first + slot], stores.at[slot])

    def source(s, slot):
        count = count_ref[s]
        for place, (which, lead) in enumerate(places):

            @pl.when((count > place) & (slot + place < slots))
            def _():
                load(which, lead, s, slot + place).start()

        return slot + count

    filled = jnp.minimum(lax.fori_loop(0, nctx, source, 0), slots)

    def blank(slot, carry):
        stage[slot] = jnp.zeros(stage.shape[1:], stage.dtype)
        store(slot).start()
        return carry

    lax.fori_loop(filled, slots, blank, 0)

    def passed(slot, carry):
        load(*places[0], 0, slot).wait()
        store(slot).start()
        return carry

    lax.fori_loop(0, filled, passed, 0)

    def finish(slot, carry):
        store(slot).wait()
        return carry

    lax.fori_loop(0, slots, finish, 0)


def unpack(count, recvs, places, cache, slots):
    rows, lanes = cache.shape[1:]
    return pl.pallas_call(
        functools.partial(unpack_kernel, places, slots),
        out_shape=jax.ShapeDtypeStruct(cache.shape, cache.dtype),
        grid_spec=pltpu.PrefetchScalarGridSpec(
            num_scalar_prefetch=1,
            grid=(1,),
            in_specs=[pl.BlockSpec(memory_space=pl.ANY)] * (len(recvs) + 1),
            out_specs=pl.BlockSpec(memory_space=pl.ANY),
            scratch_shapes=[
                pltpu.VMEM((slots, rows, lanes), cache.dtype),
                pltpu.SemaphoreType.DMA((slots,)),
                pltpu.SemaphoreType.DMA((slots,)),
            ],
        ),
        input_output_aliases={len(recvs) + 1: 0},
        cost_estimate=pl.CostEstimate(
            flops=0, bytes_accessed=4 * slots * rows * lanes, transcendentals=0
        ),
        name="unpack",
    )(count, *recvs, cache)


def attend(q, keys, values, column, limit, top, total, numer, r, log_scale):
    scores = lax.dot_general(q, keys, (((1,), (1,)), ((), ())), preferred_element_type=jnp.float32)
    scores = jnp.where(column < limit, scores, LOW)
    best = jnp.max(scores, axis=1, keepdims=True)
    best = best.astype(jnp.bfloat16).astype(jnp.float32)
    old = top[r]
    new = jnp.maximum(old, best)
    probs = jnp.exp2((scores - new[:, :1]) * log_scale)
    shrink = jnp.exp2((old - new) * log_scale)
    top[r] = new
    lanes = numer.shape[2]
    width = probs.shape[1]
    if width > lanes:
        part = probs[:, :lanes]
        for first in range(lanes, width, lanes):
            part = part + probs[:, first : first + lanes]
    else:
        part = jnp.concatenate(
            [probs, jnp.zeros((probs.shape[0], lanes - width), jnp.float32)], axis=1
        )
    total[r] = total[r] * shrink + part
    numer[r] = numer[r] * shrink + jnp.dot(
        probs.astype(jnp.bfloat16), values, preferred_element_type=jnp.float32
    )


def attention_kernel(
    kv_local, group, log_scale,
    rank_ref, req_ref, idx_ref, dst_ref, len_ref,
    q_ref, dk_ref, dv_ref, offs_ref, k_ref, v_ref,
    numer_ref, stats_ref, k_out, v_out,
    top, total, numer, column,
):
    step = pl.program_id(0)
    requests, rows, lanes = numer.shape
    width = k_ref.shape[1] // kv_local
    blocks = pl.num_programs(0) * STEP
    rank = rank_ref[0]
    base = rank * blocks + step * STEP

    @pl.when(step == 0)
    def _():
        top[...] = jnp.full(top.shape, LOW, jnp.float32)
        total[...] = jnp.zeros(total.shape, jnp.float32)
        numer[...] = jnp.zeros(numer.shape, jnp.float32)
        line = lax.broadcasted_iota(jnp.int32, column.shape, 1)
        row = lax.broadcasted_iota(jnp.int32, column.shape, 0)
        own = row % (kv_local * group) // group
        column[...] = jnp.where(line % kv_local == own, line // kv_local, 1 << 20)

        @pl.when(rank < requests)
        def _():
            drafts = dk_ref.shape[1]
            spot = column[:, :drafts]
            spot = jnp.where(spot >= offs_ref[...], spot, 1 << 20)
            token = lax.broadcasted_iota(jnp.int32, spot.shape, 0) // (kv_local * group)
            attend(q_ref[rank], dk_ref[rank], dv_ref[rank], spot, token + 1,
                   top, total, numer, rank, log_scale)

    for g in range(STEP):
        slot = base + g
        stays = dst_ref[slot] < 0

        @pl.when(stays)
        def _():
            k_out[g] = k_ref[g]
            v_out[g] = v_ref[g]

        @pl.when(jnp.logical_not(stays))
        def _():
            k_out[g] = jnp.zeros(k_out.shape[1:], k_out.dtype)
            v_out[g] = jnp.zeros(v_out.shape[1:], v_out.dtype)

        idx = idx_ref[slot]

        @pl.when(idx >= 0)
        def _():
            r = req_ref[slot]
            limit = jnp.minimum(len_ref[r] - idx * width, width)
            attend(q_ref[r], k_ref[g], v_ref[g], column[...], limit,
                   top, total, numer, r, log_scale)

    @pl.when(step == pl.num_programs(0) - 1)
    def _():
        ones = jnp.ones((8, lanes), jnp.float32)
        first = (lax.broadcasted_iota(jnp.int32, (8, lanes), 1) == 0).astype(jnp.float32)
        pick = lax.broadcasted_iota(jnp.int32, (8, rows), 0)
        turn = (((1,), (1,)), ((), ()))

        def close(r, carry):
            numer_ref[r] = numer[r].astype(numer_ref.dtype)
            sums = lax.dot_general(ones, total[r], turn, precision=lax.Precision.HIGHEST,
                                   preferred_element_type=jnp.float32)
            tops = lax.dot_general(first, top[r], turn, precision=lax.Precision.HIGHEST,
                                   preferred_element_type=jnp.float32)
            stats_ref[r] = jnp.where(pick == 0, tops, sums)
            return carry

        lax.fori_loop(0, requests, close, 0)


def attention(rank, block_req, block_idx, move_dst, lengths, q, dk, dv, offs, keys, values,
              slots, kv_local, group, log_scale):
    blocks, width, lanes = keys.shape
    requests, rows, _ = q.shape
    whole = lambda shape: pl.BlockSpec(shape, lambda i, *_: (0,) * len(shape))
    part = pl.BlockSpec((STEP, width, lanes), lambda i, *_: (i, 0, 0))
    cache = jax.ShapeDtypeStruct((blocks + slots, width, lanes), keys.dtype)
    return pl.pallas_call(
        functools.partial(attention_kernel, kv_local, group, log_scale),
        out_shape=(
            jax.ShapeDtypeStruct((requests, rows, lanes), jnp.bfloat16),
            jax.ShapeDtypeStruct((requests, 8, rows), jnp.float32),
            cache,
            cache,
        ),
        grid_spec=pltpu.PrefetchScalarGridSpec(
            num_scalar_prefetch=5,
            grid=(blocks // STEP,),
            in_specs=[whole(q.shape), whole(dk.shape), whole(dv.shape), whole(offs.shape), part, part],
            out_specs=[whole((requests, rows, lanes)), whole((requests, 8, rows)), part, part],
            scratch_shapes=[
                pltpu.VMEM((requests, rows, lanes), jnp.float32),
                pltpu.VMEM((requests, rows, lanes), jnp.float32),
                pltpu.VMEM((requests, rows, lanes), jnp.float32),
                pltpu.VMEM((rows, width), jnp.int32),
            ],
        ),
        compiler_params=pltpu.CompilerParams(vmem_limit_bytes=40 * 2**20),
        cost_estimate=pl.CostEstimate(
            flops=4 * blocks * rows * width * lanes,
            bytes_accessed=8 * blocks * width * lanes,
            transcendentals=blocks * rows * width,
        ),
        name="attention",
    )(rank, block_req, block_idx, move_dst, lengths, q, dk, dv, offs, keys, values)


def exchange(x, axis):
    return lax.all_to_all(x, axis, split_axis=0, concat_axis=0, tiled=True)


def everywhere(x, axis):
    n = lax.axis_size(axis)
    return exchange(jnp.broadcast_to(x[None], (n, *x.shape)), axis)


def shards(
    queries, draft_keys, draft_values, cache_keys, cache_values, w_out,
    lengths, block_req, block_idx, move_dst, draft_offs,
):
    blocks, width, kv_local, head_dim = cache_keys.shape
    nctx = lax.axis_size("ctx")
    rank = lax.axis_index("ctx").astype(jnp.int32)
    requests, drafts = draft_offs.shape
    own = queries.shape[0]
    heads = queries.shape[1] // head_dim
    group = heads // kv_local
    tokens = requests * drafts
    slots = nctx
    log_scale = math.log2(math.e) / math.sqrt(head_dim)
    me = rank.reshape(1)

    keys = cache_keys.reshape(blocks, width * kv_local, head_dim)
    values = cache_values.reshape(blocks, width * kv_local, head_dim)

    mine = jnp.concatenate(
        [
            queries.reshape(own * heads, head_dim),
            draft_keys.reshape(own * kv_local, head_dim),
            draft_values.reshape(own * kv_local, head_dim),
        ],
        axis=0,
    )
    lead = 128
    shared = everywhere(mine, "ctx")
    first, second, third = pack(me, move_dst, keys, values, nctx, lead)
    shared, first = lax.optimization_barrier((shared, first))
    got_keys = exchange(first, "ctx")
    cut = own * heads
    cut2 = cut + own * kv_local
    q = shared[:, :cut].reshape(requests, drafts * heads, head_dim)
    dk = shared[:, cut:cut2].reshape(requests, drafts * kv_local, head_dim)
    dv = shared[:, cut2:].reshape(requests, drafts * kv_local, head_dim)

    my_offs = lax.dynamic_slice_in_dim(draft_offs, jnp.minimum(rank, requests - 1), 1)[0]
    offs = jnp.repeat(my_offs, heads)[:, None]
    numer, stats, new_keys, new_values = attention(
        me, block_req, block_idx, move_dst, lengths, q, dk, dv, offs, keys, values,
        slots, kv_local, group, log_scale,
    )
    rows = own * heads
    tops = stats[:, 0].reshape(nctx, 1, rows)
    sums = stats[:, 1].reshape(nctx, 1, rows)
    high = sums.astype(jnp.bfloat16)
    rest = (sums - high.astype(jnp.float32)).astype(jnp.bfloat16)
    notes = jnp.concatenate([tops.astype(jnp.bfloat16), high, rest], axis=1)
    notes = jnp.pad(notes, ((0, 0), (0, 5), (0, head_dim - rows)))
    mine = jnp.concatenate([numer.reshape(nctx, rows, head_dim), notes], axis=1)
    second, got_keys = lax.optimization_barrier((second.at[:, :lead].set(mine), got_keys))
    parts = exchange(second, "ctx")
    count = jnp.sum((move_dst.reshape(nctx, blocks) == rank).astype(jnp.int32), axis=1)
    new_keys = unpack(
        count, (got_keys.reshape(nctx, -1, head_dim),),
        tuple((0, p * width * kv_local) for p in range(CAP)), new_keys, slots,
    )
    notes = parts[:, rows : rows + 3, :rows].astype(jnp.float32)
    top = jnp.max(notes[:, 0], axis=0)
    factor = jnp.exp2((notes[:, 0] - top) * log_scale)
    denom = jnp.sum(factor * (notes[:, 1] + notes[:, 2]), axis=0)
    total = jnp.sum(parts[:, :rows].astype(jnp.float32) * factor[:, :, None], axis=0)
    attn = (total / denom[:, None]).astype(jnp.bfloat16)
    fill = jnp.pad(attn, ((0, lead - rows), (0, 0)))
    third = third.at[:, :lead].set(jnp.broadcast_to(fill[None], (nctx, lead, head_dim)))
    whole = exchange(third, "ctx")
    attn = whole[:, :rows].reshape(tokens, heads * head_dim)
    partial = jnp.dot(attn, w_out, preferred_element_type=jnp.float32)
    nhead = lax.axis_size("head")
    shares = exchange(partial.reshape(nhead, tokens // nhead, -1), "head")
    mixed = functools.reduce(jnp.add, [shares[i] for i in range(nhead)]).astype(jnp.bfloat16)
    new_values = unpack(count, (parts, whole), ((0, lead), (1, lead)), new_values, slots)
    shape = (blocks + slots, width, kv_local, head_dim)
    return (mixed, new_keys.reshape(shape), new_values.reshape(shape))


def solution(mesh):
    cache = P("ctx", None, "head", None)
    in_specs = (
        P("ctx", "head"), P("ctx", "head"), P("ctx", "head"), cache, cache, P("head", "ctx"),
        P(), P(), P(), P(), P(),
    )
    out_specs = (P("head", "ctx"), cache, cache)
    return jax.shard_map(shards, mesh=mesh, in_specs=in_specs, out_specs=out_specs, check_vma=False)
```

```python
import functools
import math

import jax
import jax.numpy as jnp
from jax import lax
from jax.experimental import pallas as pl
from jax.experimental.pallas import tpu as pltpu
from jax.sharding import PartitionSpec as P

CAP = 2
STEP = 4
LOW = -1e30


def pack_kernel(rank_ref, dst_ref, k_ref, v_ref, send_ref, used, sems):
    blocks = k_ref.shape[0]
    base = rank_ref[0] * blocks

    def clear(d, carry):
        used[d] = 0
        return carry

    lax.fori_loop(0, used.shape[0], clear, 0)

    def copies(b, dst, place):
        return (
            pltpu.make_async_copy(k_ref.at[b], send_ref.at[dst, place, 0], sems.at[b, 0]),
            pltpu.make_async_copy(v_ref.at[b], send_ref.at[dst, place, 1], sems.at[b, 1]),
        )

    def start(b, carry):
        dst = dst_ref[base + b]

        @pl.when(dst >= 0)
        def _():
            place = jnp.minimum(used[dst], CAP - 1)
            used[dst] = place + 1
            for c in copies(b, dst, place):
                c.start()

        return carry

    lax.fori_loop(0, blocks, start, 0)

    def finish(b, carry):
        @pl.when(dst_ref[base + b] >= 0)
        def _():
            for c in copies(b, 0, 0):
                c.wait()

        return carry

    lax.fori_loop(0, blocks, finish, 0)


def pack(rank, move_dst, keys, values, nctx):
    blocks, rows, lanes = keys.shape
    return pl.pallas_call(
        pack_kernel,
        out_shape=jax.ShapeDtypeStruct((nctx, CAP, 2, rows, lanes), keys.dtype),
        grid_spec=pltpu.PrefetchScalarGridSpec(
            num_scalar_prefetch=2,
            grid=(1,),
            in_specs=[pl.BlockSpec((blocks, rows, lanes), lambda i, *_: (0, 0, 0))] * 2,
            out_specs=pl.BlockSpec(memory_space=pltpu.HBM),
            scratch_shapes=[
                pltpu.SMEM((nctx,), jnp.int32),
                pltpu.SemaphoreType.DMA((blocks, 2)),
            ],
        ),
        compiler_params=pltpu.CompilerParams(vmem_limit_bytes=40 * 2**20),
        cost_estimate=pl.CostEstimate(
            flops=0, bytes_accessed=4 * blocks * rows * lanes * 2, transcendentals=0
        ),
        name="pack",
    )(rank, move_dst, keys, values)


def unpack_kernel(slots, count_ref, recv_ref, _k, _v, k_out, v_out, stage, loads, stores):
    nctx = count_ref.shape[0]
    first = k_out.shape[0] - slots
    outs = (k_out, v_out)

    def load(row, place, slot, i):
        return pltpu.make_async_copy(
            recv_ref.at[row, place, i], stage.at[slot, i], loads.at[slot, i]
        )

    def store(slot, i):
        return pltpu.make_async_copy(stage.at[slot, i], outs[i].at[first + slot], stores.at[slot, i])

    def source(s, slot):
        count = count_ref[s]
        for place in range(CAP):

            @pl.when((count > place) & (slot + place < slots))
            def _():
                for i in range(2):
                    load(s, place, slot + place, i).start()

        return slot + count

    filled = jnp.minimum(lax.fori_loop(0, nctx, source, 0), slots)

    def blank(slot, carry):
        stage[slot] = jnp.zeros(stage.shape[1:], stage.dtype)
        for i in range(2):
            store(slot, i).start()
        return carry

    lax.fori_loop(filled, slots, blank, 0)

    def passed(slot, carry):
        for i in range(2):
            load(0, 0, slot, i).wait()
            store(slot, i).start()
        return carry

    lax.fori_loop(0, filled, passed, 0)

    def finish(slot, carry):
        for i in range(2):
            store(slot, i).wait()
        return carry

    lax.fori_loop(0, slots, finish, 0)


def unpack(count, recv, keys, values, slots):
    rows, lanes = keys.shape[1:]
    shape = jax.ShapeDtypeStruct(keys.shape, keys.dtype)
    return pl.pallas_call(
        functools.partial(unpack_kernel, slots),
        out_shape=(shape, shape),
        grid_spec=pltpu.PrefetchScalarGridSpec(
            num_scalar_prefetch=1,
            grid=(1,),
            in_specs=[pl.BlockSpec(memory_space=pltpu.HBM)] * 3,
            out_specs=[pl.BlockSpec(memory_space=pltpu.HBM)] * 2,
            scratch_shapes=[
                pltpu.VMEM((slots, 2, rows, lanes), keys.dtype),
                pltpu.SemaphoreType.DMA((slots, 2)),
                pltpu.SemaphoreType.DMA((slots, 2)),
            ],
        ),
        input_output_aliases={2: 0, 3: 1},
        cost_estimate=pl.CostEstimate(
            flops=0, bytes_accessed=8 * slots * rows * lanes, transcendentals=0
        ),
        name="unpack",
    )(count, recv, keys, values)


def attend(q, keys, values, column, limit, top, total, numer, r, log_scale):
    scores = lax.dot_general(q, keys, (((1,), (1,)), ((), ())), preferred_element_type=jnp.float32)
    scores = jnp.where(column < limit, scores, LOW)
    best = jnp.max(scores, axis=1, keepdims=True)
    best = best.astype(jnp.bfloat16).astype(jnp.float32)
    old = top[r]
    new = jnp.maximum(old, best)
    probs = jnp.exp2((scores - new[:, :1]) * log_scale)
    shrink = jnp.exp2((old - new) * log_scale)
    top[r] = new
    lanes = numer.shape[2]
    width = probs.shape[1]
    if width > lanes:
        part = probs[:, :lanes]
        for first in range(lanes, width, lanes):
            part = part + probs[:, first : first + lanes]
    else:
        part = jnp.concatenate(
            [probs, jnp.zeros((probs.shape[0], lanes - width), jnp.float32)], axis=1
        )
    total[r] = total[r] * shrink + part
    numer[r] = numer[r] * shrink + jnp.dot(
        probs.astype(jnp.bfloat16), values, preferred_element_type=jnp.float32
    )


def attention_kernel(
    kv_local, group, log_scale,
    rank_ref, req_ref, idx_ref, dst_ref, len_ref,
    q_ref, dk_ref, dv_ref, offs_ref, k_ref, v_ref,
    numer_ref, stats_ref, k_out, v_out,
    top, total, numer, column,
):
    step = pl.program_id(0)
    requests, rows, lanes = numer.shape
    width = k_ref.shape[1] // kv_local
    blocks = pl.num_programs(0) * STEP
    rank = rank_ref[0]
    base = rank * blocks + step * STEP

    @pl.when(step == 0)
    def _():
        top[...] = jnp.full(top.shape, LOW, jnp.float32)
        total[...] = jnp.zeros(total.shape, jnp.float32)
        numer[...] = jnp.zeros(numer.shape, jnp.float32)
        line = lax.broadcasted_iota(jnp.int32, column.shape, 1)
        row = lax.broadcasted_iota(jnp.int32, column.shape, 0)
        own = row % (kv_local * group) // group
        column[...] = jnp.where(line % kv_local == own, line // kv_local, 1 << 20)

        @pl.when(rank < requests)
        def _():
            drafts = dk_ref.shape[1]
            spot = column[:, :drafts]
            spot = jnp.where(spot >= offs_ref[...], spot, 1 << 20)
            token = lax.broadcasted_iota(jnp.int32, spot.shape, 0) // (kv_local * group)
            attend(q_ref[rank], dk_ref[rank], dv_ref[rank], spot, token + 1,
                   top, total, numer, rank, log_scale)

    for g in range(STEP):
        slot = base + g
        stays = dst_ref[slot] < 0

        @pl.when(stays)
        def _():
            k_out[g] = k_ref[g]
            v_out[g] = v_ref[g]

        @pl.when(jnp.logical_not(stays))
        def _():
            k_out[g] = jnp.zeros(k_out.shape[1:], k_out.dtype)
            v_out[g] = jnp.zeros(v_out.shape[1:], v_out.dtype)

        idx = idx_ref[slot]

        @pl.when(idx >= 0)
        def _():
            r = req_ref[slot]
            limit = jnp.minimum(len_ref[r] - idx * width, width)
            attend(q_ref[r], k_ref[g], v_ref[g], column[...], limit,
                   top, total, numer, r, log_scale)

    @pl.when(step == pl.num_programs(0) - 1)
    def _():
        ones = jnp.ones((8, lanes), jnp.float32)
        first = (lax.broadcasted_iota(jnp.int32, (8, lanes), 1) == 0).astype(jnp.float32)
        pick = lax.broadcasted_iota(jnp.int32, (8, rows), 0)
        turn = (((1,), (1,)), ((), ()))

        def close(r, carry):
            numer_ref[r] = numer[r].astype(numer_ref.dtype)
            sums = lax.dot_general(ones, total[r], turn, precision=lax.Precision.HIGHEST,
                                   preferred_element_type=jnp.float32)
            tops = lax.dot_general(first, top[r], turn, precision=lax.Precision.HIGHEST,
                                   preferred_element_type=jnp.float32)
            stats_ref[r] = jnp.where(pick == 0, tops, sums)
            return carry

        lax.fori_loop(0, requests, close, 0)


def attention(rank, block_req, block_idx, move_dst, lengths, q, dk, dv, offs, keys, values,
              slots, kv_local, group, log_scale):
    blocks, width, lanes = keys.shape
    requests, rows, _ = q.shape
    whole = lambda shape: pl.BlockSpec(shape, lambda i, *_: (0,) * len(shape))
    part = pl.BlockSpec((STEP, width, lanes), lambda i, *_: (i, 0, 0))
    cache = jax.ShapeDtypeStruct((blocks + slots, width, lanes), keys.dtype)
    return pl.pallas_call(
        functools.partial(attention_kernel, kv_local, group, log_scale),
        out_shape=(
            jax.ShapeDtypeStruct((requests, rows, lanes), jnp.float32),
            jax.ShapeDtypeStruct((requests, 8, rows), jnp.float32),
            cache,
            cache,
        ),
        grid_spec=pltpu.PrefetchScalarGridSpec(
            num_scalar_prefetch=5,
            grid=(blocks // STEP,),
            in_specs=[whole(q.shape), whole(dk.shape), whole(dv.shape), whole(offs.shape), part, part],
            out_specs=[whole((requests, rows, lanes)), whole((requests, 8, rows)), part, part],
            scratch_shapes=[
                pltpu.VMEM((requests, rows, lanes), jnp.float32),
                pltpu.VMEM((requests, rows, lanes), jnp.float32),
                pltpu.VMEM((requests, rows, lanes), jnp.float32),
                pltpu.VMEM((rows, width), jnp.int32),
            ],
        ),
        compiler_params=pltpu.CompilerParams(vmem_limit_bytes=40 * 2**20),
        cost_estimate=pl.CostEstimate(
            flops=4 * blocks * rows * width * lanes,
            bytes_accessed=8 * blocks * width * lanes,
            transcendentals=blocks * rows * width,
        ),
        name="attention",
    )(rank, block_req, block_idx, move_dst, lengths, q, dk, dv, offs, keys, values)


def exchange(x, axis, groups=None):
    return lax.all_to_all(
        x, axis, split_axis=0, concat_axis=0, tiled=True, axis_index_groups=groups
    )


def everywhere(x, axis, groups):
    return exchange(jnp.broadcast_to(x[None], (len(groups[0]), *x.shape)), axis, groups)


def across(x, axis):
    return lax.ppermute(x, axis, [(i, i ^ 1) for i in range(lax.axis_size(axis))])


def shards(
    queries, draft_keys, draft_values, cache_keys, cache_values, w_out,
    lengths, block_req, block_idx, move_dst, draft_offs,
):
    blocks, width, kv_local, head_dim = cache_keys.shape
    nctx = lax.axis_size("ctx")
    rank = lax.axis_index("ctx").astype(jnp.int32)
    requests, drafts = draft_offs.shape
    own = queries.shape[0]
    heads = queries.shape[1] // head_dim
    group = heads // kv_local
    tokens = requests * drafts
    slots = nctx
    log_scale = math.log2(math.e) / math.sqrt(head_dim)
    me = rank.reshape(1)

    keys = cache_keys.reshape(blocks, width * kv_local, head_dim)
    values = cache_values.reshape(blocks, width * kv_local, head_dim)

    mine = jnp.concatenate(
        [
            queries.reshape(own * heads, head_dim),
            draft_keys.reshape(own * kv_local, head_dim),
            draft_values.reshape(own * kv_local, head_dim),
        ],
        axis=0,
    )
    chips = nctx // 2
    odd = rank % 2 == 1
    sides = [[2 * i + side for i in range(chips)] for side in range(2)]
    send = pack(me, move_dst, keys, values, nctx)
    same = everywhere(mine, "ctx", sides)
    same, send = lax.optimization_barrier((same, send))
    recv = exchange(send, "ctx")
    other = across(same, "ctx")
    shared = jnp.where(odd, jnp.stack([other, same], axis=1), jnp.stack([same, other], axis=1))
    shared = shared.reshape(nctx, -1, head_dim)
    cut = own * heads
    cut2 = cut + own * kv_local
    q = shared[:, :cut].reshape(requests, drafts * heads, head_dim)
    dk = shared[:, cut:cut2].reshape(requests, drafts * kv_local, head_dim)
    dv = shared[:, cut2:].reshape(requests, drafts * kv_local, head_dim)

    my_offs = lax.dynamic_slice_in_dim(draft_offs, jnp.minimum(rank, requests - 1), 1)[0]
    offs = jnp.repeat(my_offs, heads)[:, None]
    numer, stats, new_keys, new_values = attention(
        me, block_req, block_idx, move_dst, lengths, q, dk, dv, offs, keys, values,
        slots, kv_local, group, log_scale,
    )
    rows = own * heads

    def halves(x):
        x = x.reshape(chips, 2, *x.shape[1:])
        return jnp.where(odd, x[:, 1], x[:, 0]), jnp.where(odd, x[:, 0], x[:, 1])

    kept, given = halves(numer.reshape(nctx, rows, head_dim))
    kept_notes, given_notes = halves(
        jnp.swapaxes(stats[:, :2], 0, 1).reshape(2, nctx, rows).swapaxes(0, 1)
    )
    taken, taken_notes = across(given, "ctx"), across(given_notes, "ctx")
    pair_top = jnp.maximum(kept_notes[:, 0], taken_notes[:, 0])
    fa = jnp.exp2((kept_notes[:, 0] - pair_top) * log_scale)
    fb = jnp.exp2((taken_notes[:, 0] - pair_top) * log_scale)
    pair = (kept * fa[:, :, None] + taken * fb[:, :, None]).astype(jnp.bfloat16)
    sums = kept_notes[:, 1] * fa + taken_notes[:, 1] * fb
    high = sums.astype(jnp.bfloat16)
    rest = (sums - high.astype(jnp.float32)).astype(jnp.bfloat16)
    notes = jnp.stack([pair_top.astype(jnp.bfloat16), high, rest], axis=1)
    notes = jnp.pad(notes, ((0, 0), (0, 5), (0, head_dim - rows)))
    packet = jnp.concatenate([pair, notes], axis=1)
    packet, recv = lax.optimization_barrier((packet, recv))
    parts = exchange(packet, "ctx", sides)
    count = jnp.sum((move_dst.reshape(nctx, blocks) == rank).astype(jnp.int32), axis=1)
    new_keys, new_values = unpack(count, recv, new_keys, new_values, slots)
    notes = parts[:, rows : rows + 3, :rows].astype(jnp.float32)
    top = jnp.max(notes[:, 0], axis=0)
    factor = jnp.exp2((notes[:, 0] - top) * log_scale)
    denom = jnp.sum(factor * (notes[:, 1] + notes[:, 2]), axis=0)
    total = jnp.sum(parts[:, :rows].astype(jnp.float32) * factor[:, :, None], axis=0)
    attn = (total / denom[:, None]).astype(jnp.bfloat16)
    same = everywhere(attn.reshape(own, heads * head_dim), "ctx", sides)
    other = across(same, "ctx")

    def project(x):
        x = x.reshape(chips * own, heads * head_dim)
        y = jnp.dot(x, w_out, preferred_element_type=jnp.float32)
        return y.reshape(chips, own, -1)

    same, other = project(same), project(other)
    partial = jnp.where(odd, jnp.stack([other, same], axis=1), jnp.stack([same, other], axis=1))
    nhead = lax.axis_size("head")
    shares = exchange(partial.reshape(nhead, tokens // nhead, -1), "head")
    mixed = functools.reduce(jnp.add, [shares[i] for i in range(nhead)]).astype(jnp.bfloat16)
    shape = (blocks + slots, width, kv_local, head_dim)
    return (mixed, new_keys.reshape(shape), new_values.reshape(shape))


def solution(mesh):
    cache = P("ctx", None, "head", None)
    in_specs = (
        P("ctx", "head"), P("ctx", "head"), P("ctx", "head"), cache, cache, P("head", "ctx"),
        P(), P(), P(), P(), P(),
    )
    out_specs = (P("head", "ctx"), cache, cache)
    return jax.shard_map(shards, mesh=mesh, in_specs=in_specs, out_specs=out_specs, check_vma=False)
```

```python
import functools
import math

import jax
import jax.numpy as jnp
from jax import lax
from jax.experimental import pallas as pl
from jax.experimental.pallas import tpu as pltpu
from jax.sharding import PartitionSpec as P

CAP = 2
STEP = 4
LOW = -1e30


def pack_kernel(rank_ref, dst_ref, k_ref, v_ref, send_ref, used, sems):
    blocks = k_ref.shape[0]
    base = rank_ref[0] * blocks

    def clear(d, carry):
        used[d] = 0
        return carry

    lax.fori_loop(0, used.shape[0], clear, 0)

    def copies(b, dst, place):
        return (
            pltpu.make_async_copy(k_ref.at[b], send_ref.at[dst, place, 0], sems.at[b, 0]),
            pltpu.make_async_copy(v_ref.at[b], send_ref.at[dst, place, 1], sems.at[b, 1]),
        )

    def start(b, carry):
        dst = dst_ref[base + b]

        @pl.when(dst >= 0)
        def _():
            place = jnp.minimum(used[dst], CAP - 1)
            used[dst] = place + 1
            for c in copies(b, dst, place):
                c.start()

        return carry

    lax.fori_loop(0, blocks, start, 0)

    def finish(b, carry):
        @pl.when(dst_ref[base + b] >= 0)
        def _():
            for c in copies(b, 0, 0):
                c.wait()

        return carry

    lax.fori_loop(0, blocks, finish, 0)


def pack(rank, move_dst, keys, values, nctx):
    blocks, rows, lanes = keys.shape
    return pl.pallas_call(
        pack_kernel,
        out_shape=jax.ShapeDtypeStruct((nctx, CAP, 2, rows, lanes), keys.dtype),
        grid_spec=pltpu.PrefetchScalarGridSpec(
            num_scalar_prefetch=2,
            grid=(1,),
            in_specs=[pl.BlockSpec((blocks, rows, lanes), lambda i, *_: (0, 0, 0))] * 2,
            out_specs=pl.BlockSpec(memory_space=pltpu.HBM),
            scratch_shapes=[
                pltpu.SMEM((nctx,), jnp.int32),
                pltpu.SemaphoreType.DMA((blocks, 2)),
            ],
        ),
        compiler_params=pltpu.CompilerParams(vmem_limit_bytes=40 * 2**20),
        cost_estimate=pl.CostEstimate(
            flops=0, bytes_accessed=4 * blocks * rows * lanes * 2, transcendentals=0
        ),
        name="pack",
    )(rank, move_dst, keys, values)


def unpack_kernel(slots, count_ref, recv_ref, _k, _v, k_out, v_out, stage, loads, stores):
    nctx = count_ref.shape[0]
    first = k_out.shape[0] - slots
    outs = (k_out, v_out)

    def load(row, place, slot, i):
        return pltpu.make_async_copy(
            recv_ref.at[row, place, i], stage.at[slot, i], loads.at[slot, i]
        )

    def store(slot, i):
        return pltpu.make_async_copy(stage.at[slot, i], outs[i].at[first + slot], stores.at[slot, i])

    def source(s, slot):
        count = count_ref[s]
        for place in range(CAP):

            @pl.when((count > place) & (slot + place < slots))
            def _():
                for i in range(2):
                    load(s, place, slot + place, i).start()

        return slot + count

    filled = jnp.minimum(lax.fori_loop(0, nctx, source, 0), slots)

    def blank(slot, carry):
        stage[slot] = jnp.zeros(stage.shape[1:], stage.dtype)
        for i in range(2):
            store(slot, i).start()
        return carry

    lax.fori_loop(filled, slots, blank, 0)

    def passed(slot, carry):
        for i in range(2):
            load(0, 0, slot, i).wait()
            store(slot, i).start()
        return carry

    lax.fori_loop(0, filled, passed, 0)

    def finish(slot, carry):
        for i in range(2):
            store(slot, i).wait()
        return carry

    lax.fori_loop(0, slots, finish, 0)


def unpack(count, recv, keys, values, slots):
    rows, lanes = keys.shape[1:]
    shape = jax.ShapeDtypeStruct(keys.shape, keys.dtype)
    return pl.pallas_call(
        functools.partial(unpack_kernel, slots),
        out_shape=(shape, shape),
        grid_spec=pltpu.PrefetchScalarGridSpec(
            num_scalar_prefetch=1,
            grid=(1,),
            in_specs=[pl.BlockSpec(memory_space=pl.ANY)] + [pl.BlockSpec(memory_space=pltpu.HBM)] * 2,
            out_specs=[pl.BlockSpec(memory_space=pltpu.HBM)] * 2,
            scratch_shapes=[
                pltpu.VMEM((slots, 2, rows, lanes), keys.dtype),
                pltpu.SemaphoreType.DMA((slots, 2)),
                pltpu.SemaphoreType.DMA((slots, 2)),
            ],
        ),
        input_output_aliases={2: 0, 3: 1},
        cost_estimate=pl.CostEstimate(
            flops=0, bytes_accessed=8 * slots * rows * lanes, transcendentals=0
        ),
        name="unpack",
    )(count, recv, keys, values)


def attend(q, keys, values, column, limit, top, total, numer, r, log_scale):
    scores = lax.dot_general(q, keys, (((1,), (1,)), ((), ())), preferred_element_type=jnp.float32)
    scores = jnp.where(column < limit, scores, LOW)
    best = jnp.max(scores, axis=1, keepdims=True)
    best = best.astype(jnp.bfloat16).astype(jnp.float32)
    old = top[r]
    new = jnp.maximum(old, best)
    probs = jnp.exp2((scores - new[:, :1]) * log_scale)
    shrink = jnp.exp2((old - new) * log_scale)
    top[r] = new
    lanes = numer.shape[2]
    width = probs.shape[1]
    if width > lanes:
        part = probs[:, :lanes]
        for first in range(lanes, width, lanes):
            part = part + probs[:, first : first + lanes]
    else:
        part = jnp.concatenate(
            [probs, jnp.zeros((probs.shape[0], lanes - width), jnp.float32)], axis=1
        )
    total[r] = total[r] * shrink + part
    high = probs.astype(jnp.bfloat16)
    rest = (probs - high.astype(jnp.float32)).astype(jnp.bfloat16)
    numer[r] = (
        numer[r] * shrink
        + jnp.dot(high, values, preferred_element_type=jnp.float32)
        + jnp.dot(rest, values, preferred_element_type=jnp.float32)
    )


def attention_kernel(
    kv_local, group, log_scale,
    rank_ref, req_ref, idx_ref, dst_ref, len_ref,
    q_ref, dk_ref, dv_ref, offs_ref, k_ref, v_ref,
    numer_ref, stats_ref, k_out, v_out,
    top, total, numer, column,
):
    step = pl.program_id(0)
    requests, rows, lanes = numer.shape
    width = k_ref.shape[1] // kv_local
    blocks = pl.num_programs(0) * STEP
    rank = rank_ref[0]
    base = rank * blocks + step * STEP

    @pl.when(step == 0)
    def _():
        top[...] = jnp.full(top.shape, LOW, jnp.float32)
        total[...] = jnp.zeros(total.shape, jnp.float32)
        numer[...] = jnp.zeros(numer.shape, jnp.float32)
        line = lax.broadcasted_iota(jnp.int32, column.shape, 1)
        row = lax.broadcasted_iota(jnp.int32, column.shape, 0)
        own = row % (kv_local * group) // group
        column[...] = jnp.where(line % kv_local == own, line // kv_local, 1 << 20)

        @pl.when(rank < requests)
        def _():
            drafts = dk_ref.shape[1]
            spot = column[:, :drafts]
            spot = jnp.where(spot >= offs_ref[...], spot, 1 << 20)
            token = lax.broadcasted_iota(jnp.int32, spot.shape, 0) // (kv_local * group)
            attend(q_ref[rank], dk_ref[rank], dv_ref[rank], spot, token + 1,
                   top, total, numer, rank, log_scale)

    for g in range(STEP):
        slot = base + g
        stays = dst_ref[slot] < 0

        @pl.when(stays)
        def _():
            k_out[g] = k_ref[g]
            v_out[g] = v_ref[g]

        @pl.when(jnp.logical_not(stays))
        def _():
            k_out[g] = jnp.zeros(k_out.shape[1:], k_out.dtype)
            v_out[g] = jnp.zeros(v_out.shape[1:], v_out.dtype)

        idx = idx_ref[slot]

        @pl.when(idx >= 0)
        def _():
            r = req_ref[slot]
            limit = jnp.minimum(len_ref[r] - idx * width, width)
            attend(q_ref[r], k_ref[g], v_ref[g], column[...], limit,
                   top, total, numer, r, log_scale)

    @pl.when(step == pl.num_programs(0) - 1)
    def _():
        ones = jnp.ones((8, lanes), jnp.float32)
        first = (lax.broadcasted_iota(jnp.int32, (8, lanes), 1) == 0).astype(jnp.float32)
        pick = lax.broadcasted_iota(jnp.int32, (8, rows), 0)
        turn = (((1,), (1,)), ((), ()))

        def close(r, carry):
            numer_ref[r] = numer[r].astype(numer_ref.dtype)
            sums = lax.dot_general(ones, total[r], turn, precision=lax.Precision.HIGHEST,
                                   preferred_element_type=jnp.float32)
            tops = lax.dot_general(first, top[r], turn, precision=lax.Precision.HIGHEST,
                                   preferred_element_type=jnp.float32)
            stats_ref[r] = jnp.where(pick == 0, tops, sums)
            return carry

        lax.fori_loop(0, requests, close, 0)


def attention(rank, block_req, block_idx, move_dst, lengths, q, dk, dv, offs, keys, values,
              slots, kv_local, group, log_scale):
    blocks, width, lanes = keys.shape
    requests, rows, _ = q.shape
    whole = lambda shape: pl.BlockSpec(shape, lambda i, *_: (0,) * len(shape))
    part = pl.BlockSpec((STEP, width, lanes), lambda i, *_: (i, 0, 0))
    cache = jax.ShapeDtypeStruct((blocks + slots, width, lanes), keys.dtype)
    return pl.pallas_call(
        functools.partial(attention_kernel, kv_local, group, log_scale),
        out_shape=(
            jax.ShapeDtypeStruct((requests, rows, lanes), jnp.float32),
            jax.ShapeDtypeStruct((requests, 8, rows), jnp.float32),
            cache,
            cache,
        ),
        grid_spec=pltpu.PrefetchScalarGridSpec(
            num_scalar_prefetch=5,
            grid=(blocks // STEP,),
            in_specs=[whole(q.shape), whole(dk.shape), whole(dv.shape), whole(offs.shape), part, part],
            out_specs=[whole((requests, rows, lanes)), whole((requests, 8, rows)), part, part],
            scratch_shapes=[
                pltpu.VMEM((requests, rows, lanes), jnp.float32),
                pltpu.VMEM((requests, rows, lanes), jnp.float32),
                pltpu.VMEM((requests, rows, lanes), jnp.float32),
                pltpu.VMEM((rows, width), jnp.int32),
            ],
        ),
        compiler_params=pltpu.CompilerParams(vmem_limit_bytes=40 * 2**20),
        cost_estimate=pl.CostEstimate(
            flops=4 * blocks * rows * width * lanes,
            bytes_accessed=8 * blocks * width * lanes,
            transcendentals=blocks * rows * width,
        ),
        name="attention",
    )(rank, block_req, block_idx, move_dst, lengths, q, dk, dv, offs, keys, values)


def exchange(x, axis, groups=None):
    return lax.all_to_all(
        x, axis, split_axis=0, concat_axis=0, tiled=True, axis_index_groups=groups
    )


def everywhere(x, axis, groups):
    return exchange(jnp.broadcast_to(x[None], (len(groups[0]), *x.shape)), axis, groups)


def around(x, axis):
    n = lax.axis_size(axis)
    here = lax.axis_index(axis)
    turns = [x] + [lax.ppermute(x, axis, [(i, (i + d) % n) for i in range(n)]) for d in range(1, n)]
    stack = jnp.stack(turns)
    return jnp.stack(
        [lax.dynamic_index_in_dim(stack, (here - i) & (n - 1), keepdims=False) for i in range(n)]
    )


def in_order(odd, same, other):
    return jnp.where(odd, jnp.stack([other, same], axis=1), jnp.stack([same, other], axis=1))


def across(x, axis):
    return lax.ppermute(x, axis, [(i, i ^ 1) for i in range(lax.axis_size(axis))])


def shards(
    queries, draft_keys, draft_values, cache_keys, cache_values, w_out,
    lengths, block_req, block_idx, move_dst, draft_offs,
):
    blocks, width, kv_local, head_dim = cache_keys.shape
    nctx = lax.axis_size("ctx")
    rank = lax.axis_index("ctx").astype(jnp.int32)
    requests, drafts = draft_offs.shape
    own = queries.shape[0]
    heads = queries.shape[1] // head_dim
    group = heads // kv_local
    tokens = requests * drafts
    slots = nctx
    log_scale = math.log2(math.e) / math.sqrt(head_dim)
    me = rank.reshape(1)

    keys = cache_keys.reshape(blocks, width * kv_local, head_dim)
    values = cache_values.reshape(blocks, width * kv_local, head_dim)

    mine = jnp.concatenate([queries, draft_keys, draft_values], axis=1)
    mine = mine.reshape(-1, head_dim)
    chips = nctx // 2
    odd = (rank & 1) == 1
    sides = [[2 * i + side for i in range(chips)] for side in range(2)]
    send = pack(me, move_dst, keys, values, nctx)
    same = everywhere(mine, "ctx", sides)
    same, send = lax.optimization_barrier((same, send))
    recv = exchange(send, "ctx")
    other = across(same, "ctx")
    shared = in_order(odd, same, other)
    shared = shared.reshape(tokens, heads + 2 * kv_local, head_dim)
    q = shared[:, :heads].reshape(requests, drafts * heads, head_dim)
    dk = shared[:, heads : heads + kv_local].reshape(requests, drafts * kv_local, head_dim)
    dv = shared[:, heads + kv_local :].reshape(requests, drafts * kv_local, head_dim)
    nhead = lax.axis_size("head")
    weights = around(w_out, "head").reshape(nhead * heads * head_dim, -1)

    my_offs = lax.dynamic_slice_in_dim(draft_offs, jnp.minimum(rank, requests - 1), 1)[0]
    offs = jnp.repeat(my_offs, heads)[:, None]
    numer, stats, new_keys, new_values = attention(
        me, block_req, block_idx, move_dst, lengths, q, dk, dv, offs, keys, values,
        slots, kv_local, group, log_scale,
    )
    each = own * heads // nhead

    def by_target(x):
        lanes = x.shape[-1]
        x = x.reshape(nhead, chips, 2, each, lanes)
        x = jnp.transpose(x, (2, 1, 0, 3, 4)).reshape(2, chips * nhead, each, lanes)
        return jnp.where(odd, x[1], x[0]), jnp.where(odd, x[0], x[1])

    kept, given = by_target(numer)
    kept_notes, given_notes = by_target(jnp.swapaxes(stats[:, :2], 1, 2))
    kept_notes, given_notes = kept_notes.swapaxes(1, 2), given_notes.swapaxes(1, 2)
    taken, taken_notes = across(given, "ctx"), across(given_notes, "ctx")
    pair_top = jnp.maximum(kept_notes[:, 0], taken_notes[:, 0])
    fa = jnp.exp2((kept_notes[:, 0] - pair_top) * log_scale)
    fb = jnp.exp2((taken_notes[:, 0] - pair_top) * log_scale)
    pair = (kept * fa[:, :, None] + taken * fb[:, :, None]).astype(jnp.bfloat16)
    sums = kept_notes[:, 1] * fa + taken_notes[:, 1] * fb
    high = sums.astype(jnp.bfloat16)
    rest = (sums - high.astype(jnp.float32)).astype(jnp.bfloat16)
    notes = jnp.concatenate([pair_top.astype(jnp.bfloat16), high, rest], axis=1)[:, None]
    notes = jnp.pad(notes, ((0, 0), (0, 1), (0, head_dim - 3 * each)))
    packet = jnp.concatenate([pair, notes], axis=1)
    packet, recv, weights = lax.optimization_barrier((packet, recv, weights))
    groups = [
        [(2 * i + side) * nhead + h for i in range(chips) for h in range(nhead)]
        for side in range(2)
    ]
    parts = exchange(packet, ("ctx", "head"), groups)
    count = jnp.sum((move_dst.reshape(nctx, blocks) == rank).astype(jnp.int32), axis=1)
    new_keys, new_values = unpack(count, recv, new_keys, new_values, slots)
    parts, new_keys, new_values = lax.optimization_barrier((parts, new_keys, new_values))
    parts = parts.reshape(chips, nhead, each + 2, head_dim)
    notes = parts[:, :, each, : 3 * each].reshape(chips, nhead, 3, each).astype(jnp.float32)
    top = jnp.max(notes[:, :, 0], axis=0)
    factor = jnp.exp2((notes[:, :, 0] - top) * log_scale)
    denom = jnp.sum(factor * (notes[:, :, 1] + notes[:, :, 2]), axis=0)
    total = jnp.sum(parts[:, :, :each].astype(jnp.float32) * factor[..., None], axis=0)
    attn = (total / denom[..., None]).astype(jnp.bfloat16)
    share = own // nhead
    line = attn.reshape(nhead, share, heads, head_dim).swapaxes(0, 1).reshape(-1, head_dim)
    same = everywhere(line, "ctx", sides)
    other = across(same, "ctx")
    full = in_order(odd, same, other).reshape(nctx * share, nhead * heads * head_dim)
    mixed = jnp.dot(full, weights, preferred_element_type=jnp.float32).astype(jnp.bfloat16)
    shape = (blocks + slots, width, kv_local, head_dim)
    return (mixed, new_keys.reshape(shape), new_values.reshape(shape))


def solution(mesh):
    cache = P("ctx", None, "head", None)
    in_specs = (
        P("ctx", "head"), P("ctx", "head"), P("ctx", "head"), cache, cache, P("head", "ctx"),
        P(), P(), P(), P(), P(),
    )
    out_specs = (P("head", "ctx"), cache, cache)
    return jax.shard_map(shards, mesh=mesh, in_specs=in_specs, out_specs=out_specs, check_vma=False)
```

```python
import functools
import math

import jax
import jax.numpy as jnp
from jax import lax
from jax.experimental import pallas as pl
from jax.experimental.pallas import tpu as pltpu
from jax.sharding import PartitionSpec as P

CAP = 2
STEP = 4
LOW = -1e30


def pack_kernel(rank_ref, dst_ref, at_ref, k_ref, v_ref, send_ref, used, sems):
    blocks = k_ref.shape[0]
    base = rank_ref[0] * blocks

    def clear(d, carry):
        used[d] = 0
        return carry

    lax.fori_loop(0, used.shape[0], clear, 0)

    def copies(b, dst, place):
        return (
            pltpu.make_async_copy(k_ref.at[b], send_ref.at[(dst * CAP + place) * 2], sems.at[b, 0]),
            pltpu.make_async_copy(v_ref.at[b], send_ref.at[(dst * CAP + place) * 2 + 1], sems.at[b, 1]),
        )

    def start(b, carry):
        dst = dst_ref[base + b]

        @pl.when(dst >= 0)
        def _():
            place = jnp.minimum(used[dst], CAP - 1)
            used[dst] = place + 1
            for c in copies(b, at_ref[dst], place):
                c.start()

        return carry

    lax.fori_loop(0, blocks, start, 0)

    def finish(b, carry):
        @pl.when(dst_ref[base + b] >= 0)
        def _():
            for c in copies(b, 0, 0):
                c.wait()

        return carry

    lax.fori_loop(0, blocks, finish, 0)


def pack(rank, move_dst, at, keys, values, nctx):
    blocks, rows, lanes = keys.shape
    return pl.pallas_call(
        pack_kernel,
        out_shape=jax.ShapeDtypeStruct((nctx * CAP * 2, rows, lanes), keys.dtype),
        grid_spec=pltpu.PrefetchScalarGridSpec(
            num_scalar_prefetch=3,
            grid=(1,),
            in_specs=[pl.BlockSpec((blocks, rows, lanes), lambda i, *_: (0, 0, 0))] * 2,
            out_specs=pl.BlockSpec(memory_space=pltpu.HBM),
            scratch_shapes=[
                pltpu.SMEM((nctx,), jnp.int32),
                pltpu.SemaphoreType.DMA((blocks, 2)),
            ],
        ),
        compiler_params=pltpu.CompilerParams(vmem_limit_bytes=40 * 2**20),
        cost_estimate=pl.CostEstimate(
            flops=0, bytes_accessed=4 * blocks * rows * lanes * 2, transcendentals=0
        ),
        name="pack",
    )(rank, move_dst, at, keys, values)


def unpack_kernel(slots, count_ref, at_ref, recv_ref, _k, _v, k_out, v_out, stage, loads, stores):
    nctx = count_ref.shape[0]
    first = k_out.shape[0] - slots
    outs = (k_out, v_out)

    def load(row, place, slot, i):
        return pltpu.make_async_copy(
            recv_ref.at[(row * CAP + place) * 2 + i], stage.at[slot, i], loads.at[slot, i]
        )

    def store(slot, i):
        return pltpu.make_async_copy(stage.at[slot, i], outs[i].at[first + slot], stores.at[slot, i])

    def source(s, slot):
        count = count_ref[s]
        for place in range(CAP):

            @pl.when((count > place) & (slot + place < slots))
            def _():
                for i in range(2):
                    load(at_ref[s], place, slot + place, i).start()

        return slot + count

    filled = jnp.minimum(lax.fori_loop(0, nctx, source, 0), slots)

    def blank(slot, carry):
        stage[slot] = jnp.zeros(stage.shape[1:], stage.dtype)
        for i in range(2):
            store(slot, i).start()
        return carry

    lax.fori_loop(filled, slots, blank, 0)

    def passed(slot, carry):
        for i in range(2):
            load(0, 0, slot, i).wait()
            store(slot, i).start()
        return carry

    lax.fori_loop(0, filled, passed, 0)

    def finish(slot, carry):
        for i in range(2):
            store(slot, i).wait()
        return carry

    lax.fori_loop(0, slots, finish, 0)


def unpack(count, at, recv, keys, values, slots):
    rows, lanes = keys.shape[1:]
    shape = jax.ShapeDtypeStruct(keys.shape, keys.dtype)
    return pl.pallas_call(
        functools.partial(unpack_kernel, slots),
        out_shape=(shape, shape),
        grid_spec=pltpu.PrefetchScalarGridSpec(
            num_scalar_prefetch=2,
            grid=(1,),
            in_specs=[pl.BlockSpec(memory_space=pl.ANY)] + [pl.BlockSpec(memory_space=pltpu.HBM)] * 2,
            out_specs=[pl.BlockSpec(memory_space=pltpu.HBM)] * 2,
            scratch_shapes=[
                pltpu.VMEM((slots, 2, rows, lanes), keys.dtype),
                pltpu.SemaphoreType.DMA((slots, 2)),
                pltpu.SemaphoreType.DMA((slots, 2)),
            ],
        ),
        input_output_aliases={3: 0, 4: 1},
        cost_estimate=pl.CostEstimate(
            flops=0, bytes_accessed=8 * slots * rows * lanes, transcendentals=0
        ),
        name="unpack",
    )(count, at, recv, keys, values)


def attend(q, keys, values, column, limit, top, total, numer, r, log_scale):
    scores = lax.dot_general(q, keys, (((1,), (1,)), ((), ())), preferred_element_type=jnp.float32)
    scores = jnp.where(column < limit, scores, LOW)
    best = jnp.max(scores, axis=1, keepdims=True)
    best = best.astype(jnp.bfloat16).astype(jnp.float32)
    old = top[r]
    new = jnp.maximum(old, best)
    probs = jnp.exp2((scores - new[:, :1]) * log_scale)
    shrink = jnp.exp2((old - new) * log_scale)
    top[r] = new
    lanes = numer.shape[2]
    width = probs.shape[1]
    if width > lanes:
        part = probs[:, :lanes]
        for first in range(lanes, width, lanes):
            part = part + probs[:, first : first + lanes]
    else:
        part = jnp.concatenate(
            [probs, jnp.zeros((probs.shape[0], lanes - width), jnp.float32)], axis=1
        )
    total[r] = total[r] * shrink + part
    high = probs.astype(jnp.bfloat16)
    rest = (probs - high.astype(jnp.float32)).astype(jnp.bfloat16)
    numer[r] = (
        numer[r] * shrink
        + jnp.dot(high, values, preferred_element_type=jnp.float32)
        + jnp.dot(rest, values, preferred_element_type=jnp.float32)
    )


def attention_kernel(
    kv_local, group, log_scale,
    rank_ref, req_ref, idx_ref, dst_ref, len_ref,
    q_ref, dk_ref, dv_ref, offs_ref, k_ref, v_ref,
    numer_ref, stats_ref, k_out, v_out,
    top, total, numer, column,
):
    step = pl.program_id(0)
    requests, rows, lanes = numer.shape
    width = k_ref.shape[1] // kv_local
    blocks = pl.num_programs(0) * STEP
    rank = rank_ref[0]
    base = rank * blocks + step * STEP

    @pl.when(step == 0)
    def _():
        top[...] = jnp.full(top.shape, LOW, jnp.float32)
        total[...] = jnp.zeros(total.shape, jnp.float32)
        numer[...] = jnp.zeros(numer.shape, jnp.float32)
        line = lax.broadcasted_iota(jnp.int32, column.shape, 1)
        row = lax.broadcasted_iota(jnp.int32, column.shape, 0)
        own = row % (kv_local * group) // group
        column[...] = jnp.where(line % kv_local == own, line // kv_local, 1 << 20)

        @pl.when(rank < requests)
        def _():
            drafts = dk_ref.shape[1]
            spot = column[:, :drafts]
            spot = jnp.where(spot >= offs_ref[...], spot, 1 << 20)
            token = lax.broadcasted_iota(jnp.int32, spot.shape, 0) // (kv_local * group)
            attend(q_ref[rank], dk_ref[rank], dv_ref[rank], spot, token + 1,
                   top, total, numer, rank, log_scale)

    for g in range(STEP):
        slot = base + g
        stays = dst_ref[slot] < 0

        @pl.when(stays)
        def _():
            k_out[g] = k_ref[g]
            v_out[g] = v_ref[g]

        @pl.when(jnp.logical_not(stays))
        def _():
            k_out[g] = jnp.zeros(k_out.shape[1:], k_out.dtype)
            v_out[g] = jnp.zeros(v_out.shape[1:], v_out.dtype)

        idx = idx_ref[slot]

        @pl.when(idx >= 0)
        def _():
            r = req_ref[slot]
            limit = jnp.minimum(len_ref[r] - idx * width, width)
            attend(q_ref[r], k_ref[g], v_ref[g], column[...], limit,
                   top, total, numer, r, log_scale)

    @pl.when(step == pl.num_programs(0) - 1)
    def _():
        ones = jnp.ones((8, lanes), jnp.float32)
        first = (lax.broadcasted_iota(jnp.int32, (8, lanes), 1) == 0).astype(jnp.float32)
        pick = lax.broadcasted_iota(jnp.int32, (8, rows), 0)
        turn = (((1,), (1,)), ((), ()))

        def close(r, carry):
            numer_ref[r] = numer[r].astype(numer_ref.dtype)
            sums = lax.dot_general(ones, total[r], turn, precision=lax.Precision.HIGHEST,
                                   preferred_element_type=jnp.float32)
            tops = lax.dot_general(first, top[r], turn, precision=lax.Precision.HIGHEST,
                                   preferred_element_type=jnp.float32)
            stats_ref[r] = jnp.where(pick == 0, tops, sums)
            return carry

        lax.fori_loop(0, requests, close, 0)


def attention(rank, block_req, block_idx, move_dst, lengths, q, dk, dv, offs, keys, values,
              slots, kv_local, group, log_scale):
    blocks, width, lanes = keys.shape
    requests, rows, _ = q.shape
    whole = lambda shape: pl.BlockSpec(shape, lambda i, *_: (0,) * len(shape))
    part = pl.BlockSpec((STEP, width, lanes), lambda i, *_: (i, 0, 0))
    cache = jax.ShapeDtypeStruct((blocks + slots, width, lanes), keys.dtype)
    return pl.pallas_call(
        functools.partial(attention_kernel, kv_local, group, log_scale),
        out_shape=(
            jax.ShapeDtypeStruct((requests, rows, lanes), jnp.float32),
            jax.ShapeDtypeStruct((requests, 8, rows), jnp.float32),
            cache,
            cache,
        ),
        grid_spec=pltpu.PrefetchScalarGridSpec(
            num_scalar_prefetch=5,
            grid=(blocks // STEP,),
            in_specs=[whole(q.shape), whole(dk.shape), whole(dv.shape), whole(offs.shape), part, part],
            out_specs=[whole((requests, rows, lanes)), whole((requests, 8, rows)), part, part],
            scratch_shapes=[
                pltpu.VMEM((requests, rows, lanes), jnp.float32),
                pltpu.VMEM((requests, rows, lanes), jnp.float32),
                pltpu.VMEM((requests, rows, lanes), jnp.float32),
                pltpu.VMEM((rows, width), jnp.int32),
            ],
        ),
        compiler_params=pltpu.CompilerParams(vmem_limit_bytes=40 * 2**20),
        cost_estimate=pl.CostEstimate(
            flops=4 * blocks * rows * width * lanes,
            bytes_accessed=8 * blocks * width * lanes,
            transcendentals=blocks * rows * width,
        ),
        name="attention",
    )(rank, block_req, block_idx, move_dst, lengths, q, dk, dv, offs, keys, values)


def settle_kernel(x_ref, out_ref):
    out_ref[...] = x_ref[...]


def settle(x):
    return pl.pallas_call(
        settle_kernel, out_shape=jax.ShapeDtypeStruct(x.shape, x.dtype), name="settle"
    )(x)


def exchange(x, axis, groups=None):
    return lax.all_to_all(
        x, axis, split_axis=0, concat_axis=0, tiled=True, axis_index_groups=groups
    )


def everywhere(x, axis, groups):
    return exchange(jnp.broadcast_to(x[None], (len(groups[0]), *x.shape)), axis, groups)


def around(x, axis):
    n = lax.axis_size(axis)
    here = lax.axis_index(axis)
    turns = [x] + [lax.ppermute(x, axis, [(i, (i + d) % n) for i in range(n)]) for d in range(1, n)]
    stack = jnp.stack(turns)
    return jnp.stack(
        [lax.dynamic_index_in_dim(stack, (here - i) & (n - 1), keepdims=False) for i in range(n)]
    )


def in_order(odd, same, other):
    return jnp.where(odd, jnp.stack([other, same], axis=1), jnp.stack([same, other], axis=1))


def across(x, axis):
    return lax.ppermute(x, axis, [(i, i ^ 1) for i in range(lax.axis_size(axis))])


def shards(
    queries, draft_keys, draft_values, cache_keys, cache_values, w_out,
    lengths, block_req, block_idx, move_dst, draft_offs,
):
    blocks, width, kv_local, head_dim = cache_keys.shape
    nctx = lax.axis_size("ctx")
    rank = lax.axis_index("ctx").astype(jnp.int32)
    requests, drafts = draft_offs.shape
    own = queries.shape[0]
    heads = queries.shape[1] // head_dim
    group = heads // kv_local
    tokens = requests * drafts
    slots = nctx
    log_scale = math.log2(math.e) / math.sqrt(head_dim)
    me = rank.reshape(1)

    keys = cache_keys.reshape(blocks, width * kv_local, head_dim)
    values = cache_values.reshape(blocks, width * kv_local, head_dim)

    mine = jnp.concatenate([queries, draft_keys, draft_values], axis=1)
    mine = mine.reshape(-1, head_dim)
    chips = nctx // 2
    odd = (rank & 1) == 1
    sides = [[2 * i + side for i in range(chips)] for side in range(2)]
    order = [(d + x) % 4 * 8 + x * 2 + c for d in range(4) for x in range(4) for c in range(2)]
    at = jnp.asarray([order.index(i) for i in range(nctx)], jnp.int32)
    send = pack(me, move_dst, at, keys, values, nctx)
    same = everywhere(mine, "ctx", sides)
    same, send = lax.optimization_barrier((same, send))
    recv = exchange(send, "ctx", [order])
    other = across(same, "ctx")
    shared = in_order(odd, same, other)
    shared = shared.reshape(tokens, heads + 2 * kv_local, head_dim)
    q = shared[:, :heads].reshape(requests, drafts * heads, head_dim)
    dk = shared[:, heads : heads + kv_local].reshape(requests, drafts * kv_local, head_dim)
    dv = shared[:, heads + kv_local :].reshape(requests, drafts * kv_local, head_dim)
    nhead = lax.axis_size("head")
    weights = around(w_out, "head").reshape(nhead * heads * head_dim, -1)

    my_offs = lax.dynamic_slice_in_dim(draft_offs, jnp.minimum(rank, requests - 1), 1)[0]
    offs = jnp.repeat(my_offs, heads)[:, None]
    numer, stats, new_keys, new_values = attention(
        me, block_req, block_idx, move_dst, lengths, q, dk, dv, offs, keys, values,
        slots, kv_local, group, log_scale,
    )
    each = own * heads // nhead

    def by_target(x):
        lanes = x.shape[-1]
        x = x.reshape(nhead, chips, 2, each, lanes)
        x = jnp.transpose(x, (2, 1, 0, 3, 4)).reshape(2, chips * nhead, each, lanes)
        return jnp.where(odd, x[1], x[0]), jnp.where(odd, x[0], x[1])

    kept, given = by_target(numer)
    kept_notes, given_notes = by_target(jnp.swapaxes(stats[:, :2], 1, 2))
    kept_notes, given_notes = kept_notes.swapaxes(1, 2), given_notes.swapaxes(1, 2)
    taken, taken_notes = across(given, "ctx"), across(given_notes, "ctx")
    pair_top = jnp.maximum(kept_notes[:, 0], taken_notes[:, 0])
    fa = jnp.exp2((kept_notes[:, 0] - pair_top) * log_scale)
    fb = jnp.exp2((taken_notes[:, 0] - pair_top) * log_scale)
    pair = (kept * fa[:, :, None] + taken * fb[:, :, None]).astype(jnp.bfloat16)
    sums = kept_notes[:, 1] * fa + taken_notes[:, 1] * fb
    high = sums.astype(jnp.bfloat16)
    rest = (sums - high.astype(jnp.float32)).astype(jnp.bfloat16)
    notes = jnp.concatenate([pair_top.astype(jnp.bfloat16), high, rest], axis=1)[:, None]
    notes = jnp.pad(notes, ((0, 0), (0, 1), (0, head_dim - 3 * each)))
    packet = jnp.concatenate([pair, notes], axis=1)
    packet = settle(packet)
    packet, recv, weights = lax.optimization_barrier((packet, recv, weights))
    groups = [
        [(2 * i + side) * nhead + h for i in range(chips) for h in range(nhead)]
        for side in range(2)
    ]
    parts = exchange(packet, ("ctx", "head"), groups)
    count = jnp.sum((move_dst.reshape(nctx, blocks) == rank).astype(jnp.int32), axis=1)
    new_keys, new_values = unpack(count, at, recv, new_keys, new_values, slots)
    parts, new_keys, new_values = lax.optimization_barrier((parts, new_keys, new_values))
    parts = parts.reshape(chips, nhead, each + 2, head_dim)
    notes = parts[:, :, each, : 3 * each].reshape(chips, nhead, 3, each).astype(jnp.float32)
    top = jnp.max(notes[:, :, 0], axis=0)
    factor = jnp.exp2((notes[:, :, 0] - top) * log_scale)
    denom = jnp.sum(factor * (notes[:, :, 1] + notes[:, :, 2]), axis=0)
    total = jnp.sum(parts[:, :, :each].astype(jnp.float32) * factor[..., None], axis=0)
    attn = (total / denom[..., None]).astype(jnp.bfloat16)
    share = own // nhead
    line = attn.reshape(nhead, share, heads, head_dim).swapaxes(0, 1).reshape(-1, head_dim)
    same = everywhere(line, "ctx", sides)
    other = across(same, "ctx")

    def project(x):
        x = x.reshape(chips * share, nhead * heads * head_dim)
        y = jnp.dot(x, weights, preferred_element_type=jnp.float32).astype(jnp.bfloat16)
        return y.reshape(chips, share, -1)

    mixed = in_order(odd, project(same), project(other)).reshape(nctx * share, -1)
    shape = (blocks + slots, width, kv_local, head_dim)
    return (mixed, new_keys.reshape(shape), new_values.reshape(shape))


def solution(mesh):
    cache = P("ctx", None, "head", None)
    in_specs = (
        P("ctx", "head"), P("ctx", "head"), P("ctx", "head"), cache, cache, P("head", "ctx"),
        P(), P(), P(), P(), P(),
    )
    out_specs = (P("head", "ctx"), cache, cache)
    return jax.shard_map(shards, mesh=mesh, in_specs=in_specs, out_specs=out_specs, check_vma=False)
```

```python
import functools
import math

import jax
import jax.numpy as jnp
from jax import lax
from jax.experimental import pallas as pl
from jax.experimental.pallas import tpu as pltpu
from jax.sharding import PartitionSpec as P

CAP = 2
STEP = 4
SHIFT = 8
LOW = -1e30


def pack_kernel(rank_ref, dst_ref, at_ref, k_ref, v_ref, send_ref, used, sems):
    blocks = k_ref.shape[0]
    base = rank_ref[0] * blocks

    def clear(d, carry):
        used[d] = 0
        return carry

    lax.fori_loop(0, used.shape[0], clear, 0)

    def copies(b, dst, place):
        return (
            pltpu.make_async_copy(k_ref.at[b], send_ref.at[(dst * CAP + place) * 2], sems.at[b, 0]),
            pltpu.make_async_copy(v_ref.at[b], send_ref.at[(dst * CAP + place) * 2 + 1], sems.at[b, 1]),
        )

    def start(b, carry):
        dst = dst_ref[base + b]

        @pl.when(dst >= 0)
        def _():
            place = jnp.minimum(used[dst], CAP - 1)
            used[dst] = place + 1
            for c in copies(b, at_ref[dst], place):
                c.start()

        return carry

    lax.fori_loop(0, blocks, start, 0)

    def finish(b, carry):
        @pl.when(dst_ref[base + b] >= 0)
        def _():
            for c in copies(b, 0, 0):
                c.wait()

        return carry

    lax.fori_loop(0, blocks, finish, 0)


def pack(rank, move_dst, at, keys, values, nctx):
    blocks, rows, lanes = keys.shape
    return pl.pallas_call(
        pack_kernel,
        out_shape=jax.ShapeDtypeStruct((nctx * CAP * 2, rows, lanes), keys.dtype),
        grid_spec=pltpu.PrefetchScalarGridSpec(
            num_scalar_prefetch=3,
            grid=(1,),
            in_specs=[pl.BlockSpec((blocks, rows, lanes), lambda i, *_: (0, 0, 0))] * 2,
            out_specs=pl.BlockSpec(memory_space=pltpu.HBM),
            scratch_shapes=[
                pltpu.SMEM((nctx,), jnp.int32),
                pltpu.SemaphoreType.DMA((blocks, 2)),
            ],
        ),
        compiler_params=pltpu.CompilerParams(vmem_limit_bytes=40 * 2**20),
        cost_estimate=pl.CostEstimate(
            flops=0, bytes_accessed=4 * blocks * rows * lanes * 2, transcendentals=0
        ),
        name="pack",
    )(rank, move_dst, at, keys, values)


def unpack_kernel(slots, count_ref, at_ref, recv_ref, _k, _v, k_out, v_out, stage, loads, stores):
    nctx = count_ref.shape[0]
    first = k_out.shape[0] - slots
    outs = (k_out, v_out)

    def load(row, place, slot, i):
        return pltpu.make_async_copy(
            recv_ref.at[(row * CAP + place) * 2 + i], stage.at[slot, i], loads.at[slot, i]
        )

    def store(slot, i):
        return pltpu.make_async_copy(stage.at[slot, i], outs[i].at[first + slot], stores.at[slot, i])

    def source(s, slot):
        count = count_ref[s]
        for place in range(CAP):

            @pl.when((count > place) & (slot + place < slots))
            def _():
                for i in range(2):
                    load(at_ref[s], place, slot + place, i).start()

        return slot + count

    filled = jnp.minimum(lax.fori_loop(0, nctx, source, 0), slots)

    def blank(slot, carry):
        stage[slot] = jnp.zeros(stage.shape[1:], stage.dtype)
        for i in range(2):
            store(slot, i).start()
        return carry

    lax.fori_loop(filled, slots, blank, 0)

    def passed(slot, carry):
        for i in range(2):
            load(0, 0, slot, i).wait()
            store(slot, i).start()
        return carry

    lax.fori_loop(0, filled, passed, 0)

    def finish(slot, carry):
        for i in range(2):
            store(slot, i).wait()
        return carry

    lax.fori_loop(0, slots, finish, 0)


def unpack(count, at, recv, keys, values, slots):
    rows, lanes = keys.shape[1:]
    shape = jax.ShapeDtypeStruct(keys.shape, keys.dtype)
    return pl.pallas_call(
        functools.partial(unpack_kernel, slots),
        out_shape=(shape, shape),
        grid_spec=pltpu.PrefetchScalarGridSpec(
            num_scalar_prefetch=2,
            grid=(1,),
            in_specs=[pl.BlockSpec(memory_space=pl.ANY)] + [pl.BlockSpec(memory_space=pltpu.HBM)] * 2,
            out_specs=[pl.BlockSpec(memory_space=pltpu.HBM)] * 2,
            scratch_shapes=[
                pltpu.VMEM((slots, 2, rows, lanes), keys.dtype),
                pltpu.SemaphoreType.DMA((slots, 2)),
                pltpu.SemaphoreType.DMA((slots, 2)),
            ],
        ),
        input_output_aliases={3: 0, 4: 1},
        cost_estimate=pl.CostEstimate(
            flops=0, bytes_accessed=8 * slots * rows * lanes, transcendentals=0
        ),
        name="unpack",
    )(count, at, recv, keys, values)


def attend(q, keys, values, column, limit, top, total, numer, r, log_scale):
    scores = lax.dot_general(q, keys, (((1,), (1,)), ((), ())), preferred_element_type=jnp.float32)
    scores = jnp.where(column < limit, scores, LOW)
    best = jnp.max(scores, axis=1, keepdims=True)
    best = best.astype(jnp.bfloat16).astype(jnp.float32)
    old = top[r]
    new = jnp.maximum(old, best)
    probs = jnp.exp2((scores - new[:, :1]) * log_scale)
    shrink = jnp.exp2((old - new) * log_scale)
    top[r] = new
    lanes = numer.shape[2]
    width = probs.shape[1]
    if width > lanes:
        part = probs[:, :lanes]
        for first in range(lanes, width, lanes):
            part = part + probs[:, first : first + lanes]
    else:
        part = jnp.concatenate(
            [probs, jnp.zeros((probs.shape[0], lanes - width), jnp.float32)], axis=1
        )
    total[r] = total[r] * shrink + part
    high = probs.astype(jnp.bfloat16)
    rest = (probs - high.astype(jnp.float32)).astype(jnp.bfloat16)
    numer[r] = (
        numer[r] * shrink
        + jnp.dot(high, values, preferred_element_type=jnp.float32)
        + jnp.dot(rest, values, preferred_element_type=jnp.float32)
    )


def attention_kernel(
    kv_local, group, log_scale,
    rank_ref, req_ref, idx_ref, dst_ref, len_ref,
    q_ref, dk_ref, dv_ref, offs_ref, k_ref, v_ref,
    numer_ref, stats_ref, k_out, v_out,
    top, total, numer, column,
):
    step = pl.program_id(0)
    requests, rows, lanes = numer.shape
    width = k_ref.shape[1] // kv_local
    blocks = pl.num_programs(0) * STEP
    rank = rank_ref[0]
    base = rank * blocks + step * STEP

    @pl.when(step == 0)
    def _():
        top[...] = jnp.full(top.shape, LOW, jnp.float32)
        total[...] = jnp.zeros(total.shape, jnp.float32)
        numer[...] = jnp.zeros(numer.shape, jnp.float32)
        line = lax.broadcasted_iota(jnp.int32, column.shape, 1)
        row = lax.broadcasted_iota(jnp.int32, column.shape, 0)
        own = row % (kv_local * group) // group
        column[...] = jnp.where(line % kv_local == own, line // kv_local, 1 << 20)

        @pl.when(rank < requests)
        def _():
            drafts = dk_ref.shape[1]
            spot = column[:, :drafts]
            spot = jnp.where(spot >= offs_ref[...], spot, 1 << 20)
            token = lax.broadcasted_iota(jnp.int32, spot.shape, 0) // (kv_local * group)
            attend(q_ref[rank], dk_ref[rank], dv_ref[rank], spot, token + 1,
                   top, total, numer, rank, log_scale)

    for g in range(STEP):
        slot = base + g
        stays = dst_ref[slot] < 0

        @pl.when(stays)
        def _():
            k_out[g] = k_ref[g]
            v_out[g] = v_ref[g]

        @pl.when(jnp.logical_not(stays))
        def _():
            k_out[g] = jnp.zeros(k_out.shape[1:], k_out.dtype)
            v_out[g] = jnp.zeros(v_out.shape[1:], v_out.dtype)

        idx = idx_ref[slot]

        @pl.when(idx >= 0)
        def _():
            r = req_ref[slot]
            limit = jnp.minimum(len_ref[r] - idx * width, width)
            attend(q_ref[r], k_ref[g], v_ref[g], column[...], limit,
                   top, total, numer, r, log_scale)

    @pl.when(step == pl.num_programs(0) - 1)
    def _():
        ones = jnp.ones((8, lanes), jnp.float32)
        first = (lax.broadcasted_iota(jnp.int32, (8, lanes), 1) == 0).astype(jnp.float32)
        pick = lax.broadcasted_iota(jnp.int32, (8, rows), 0)
        turn = (((1,), (1,)), ((), ()))

        def close(r, carry):
            numer_ref[r] = numer[r].astype(numer_ref.dtype)
            sums = lax.dot_general(ones, total[r], turn, precision=lax.Precision.HIGHEST,
                                   preferred_element_type=jnp.float32)
            tops = lax.dot_general(first, top[r], turn, precision=lax.Precision.HIGHEST,
                                   preferred_element_type=jnp.float32)
            stats_ref[r] = jnp.where(pick == 0, tops, sums)
            return carry

        lax.fori_loop(0, requests, close, 0)


def attention(rank, block_req, block_idx, move_dst, lengths, q, dk, dv, offs, keys, values,
              slots, kv_local, group, log_scale):
    blocks, width, lanes = keys.shape
    requests, rows, _ = q.shape
    whole = lambda shape: pl.BlockSpec(shape, lambda i, *_: (0,) * len(shape))
    part = pl.BlockSpec((STEP, width, lanes), lambda i, *_: (i, 0, 0))
    cache = jax.ShapeDtypeStruct((blocks + slots, width, lanes), keys.dtype)
    return pl.pallas_call(
        functools.partial(attention_kernel, kv_local, group, log_scale),
        out_shape=(
            jax.ShapeDtypeStruct((requests, rows, lanes), jnp.float32),
            jax.ShapeDtypeStruct((requests, 8, rows), jnp.float32),
            cache,
            cache,
        ),
        grid_spec=pltpu.PrefetchScalarGridSpec(
            num_scalar_prefetch=5,
            grid=(blocks // STEP,),
            in_specs=[whole(q.shape), whole(dk.shape), whole(dv.shape), whole(offs.shape), part, part],
            out_specs=[whole((requests, rows, lanes)), whole((requests, 8, rows)), part, part],
            scratch_shapes=[
                pltpu.VMEM((requests, rows, lanes), jnp.float32),
                pltpu.VMEM((requests, rows, lanes), jnp.float32),
                pltpu.VMEM((requests, rows, lanes), jnp.float32),
                pltpu.VMEM((rows, width), jnp.int32),
            ],
        ),
        compiler_params=pltpu.CompilerParams(vmem_limit_bytes=40 * 2**20),
        cost_estimate=pl.CostEstimate(
            flops=4 * blocks * rows * width * lanes,
            bytes_accessed=8 * blocks * width * lanes,
            transcendentals=blocks * rows * width,
        ),
        name="attention",
    )(rank, block_req, block_idx, move_dst, lengths, q, dk, dv, offs, keys, values)


def settle_kernel(x_ref, out_ref):
    out_ref[...] = x_ref[...]


def settle(x):
    return pl.pallas_call(
        settle_kernel, out_shape=jax.ShapeDtypeStruct(x.shape, x.dtype), name="settle"
    )(x)


def exchange(x, axis, groups=None):
    return lax.all_to_all(
        x, axis, split_axis=0, concat_axis=0, tiled=True, axis_index_groups=groups
    )


def everywhere(x, axis, groups):
    return exchange(jnp.broadcast_to(x[None], (len(groups[0]), *x.shape)), axis, groups)


def around(x, axis):
    n = lax.axis_size(axis)
    here = lax.axis_index(axis)
    turns = [x] + [lax.ppermute(x, axis, [(i, (i + d) % n) for i in range(n)]) for d in range(1, n)]
    stack = jnp.stack(turns)
    return jnp.stack(
        [lax.dynamic_index_in_dim(stack, (here - i) & (n - 1), keepdims=False) for i in range(n)]
    )


def rotate(x, by):
    return jnp.concatenate([x[by:], x[:by]], axis=0)


def in_order(odd, same, other):
    even_rows, odd_rows = jnp.where(odd, other, same), jnp.where(odd, same, other)
    return jnp.stack([even_rows, rotate(odd_rows, -SHIFT)], axis=1)


def across(x, axis):
    return lax.ppermute(x, axis, [(i, i ^ 1) for i in range(lax.axis_size(axis))])


def shards(
    queries, draft_keys, draft_values, cache_keys, cache_values, w_out,
    lengths, block_req, block_idx, move_dst, draft_offs,
):
    blocks, width, kv_local, head_dim = cache_keys.shape
    nctx = lax.axis_size("ctx")
    rank = lax.axis_index("ctx").astype(jnp.int32)
    requests, drafts = draft_offs.shape
    own = queries.shape[0]
    heads = queries.shape[1] // head_dim
    group = heads // kv_local
    tokens = requests * drafts
    slots = nctx
    log_scale = math.log2(math.e) / math.sqrt(head_dim)
    me = rank.reshape(1)

    keys = cache_keys.reshape(blocks, width * kv_local, head_dim)
    values = cache_values.reshape(blocks, width * kv_local, head_dim)

    mine = jnp.concatenate([queries, draft_keys, draft_values], axis=1)
    mine = mine.reshape(-1, head_dim)
    chips = nctx // 2
    odd = (rank & 1) == 1
    rings = [[(i + side * SHIFT) % chips for i in range(chips)] for side in range(2)]
    sides = [[2 * i + side for i in rings[side]] for side in range(2)]
    order = [(d + x) % 4 * 8 + x * 2 + c for d in range(4) for x in range(4) for c in range(2)]
    at = jnp.asarray([order.index(i) for i in range(nctx)], jnp.int32)
    send = pack(me, move_dst, at, keys, values, nctx)
    same = everywhere(mine, "ctx", sides)
    same, send = lax.optimization_barrier((same, send))
    recv = exchange(send, "ctx", [order])
    other = across(same, "ctx")
    shared = in_order(odd, same, other)
    shared = shared.reshape(tokens, heads + 2 * kv_local, head_dim)
    q = shared[:, :heads].reshape(requests, drafts * heads, head_dim)
    dk = shared[:, heads : heads + kv_local].reshape(requests, drafts * kv_local, head_dim)
    dv = shared[:, heads + kv_local :].reshape(requests, drafts * kv_local, head_dim)
    nhead = lax.axis_size("head")
    weights = around(w_out, "head").reshape(nhead * heads * head_dim, -1)

    my_offs = lax.dynamic_slice_in_dim(draft_offs, jnp.minimum(rank, requests - 1), 1)[0]
    offs = jnp.repeat(my_offs, heads)[:, None]
    numer, stats, new_keys, new_values = attention(
        me, block_req, block_idx, move_dst, lengths, q, dk, dv, offs, keys, values,
        slots, kv_local, group, log_scale,
    )
    each = own * heads // nhead

    def by_target(x):
        lanes = x.shape[-1]
        x = x.reshape(nhead, chips, 2, each, lanes)
        x = jnp.transpose(x, (2, 1, 0, 3, 4)).reshape(2, chips * nhead, each, lanes)
        even_rows, odd_rows = x[0], rotate(x[1], SHIFT * nhead)
        return jnp.where(odd, odd_rows, even_rows), jnp.where(odd, even_rows, odd_rows)

    kept, given = by_target(numer)
    kept_notes, given_notes = by_target(jnp.swapaxes(stats[:, :2], 1, 2))
    kept_notes, given_notes = kept_notes.swapaxes(1, 2), given_notes.swapaxes(1, 2)
    taken, taken_notes = across(given, "ctx"), across(given_notes, "ctx")
    pair_top = jnp.maximum(kept_notes[:, 0], taken_notes[:, 0])
    fa = jnp.exp2((kept_notes[:, 0] - pair_top) * log_scale)
    fb = jnp.exp2((taken_notes[:, 0] - pair_top) * log_scale)
    pair = (kept * fa[:, :, None] + taken * fb[:, :, None]).astype(jnp.bfloat16)
    sums = kept_notes[:, 1] * fa + taken_notes[:, 1] * fb
    high = sums.astype(jnp.bfloat16)
    rest = (sums - high.astype(jnp.float32)).astype(jnp.bfloat16)
    notes = jnp.concatenate([pair_top.astype(jnp.bfloat16), high, rest], axis=1)[:, None]
    notes = jnp.pad(notes, ((0, 0), (0, 1), (0, head_dim - 3 * each)))
    packet = jnp.concatenate([pair, notes], axis=1)
    packet = settle(packet)
    packet, recv, weights = lax.optimization_barrier((packet, recv, weights))
    groups = [
        [(2 * i + side) * nhead + h for i in rings[side] for h in range(nhead)]
        for side in range(2)
    ]
    parts = exchange(packet, ("ctx", "head"), groups)
    count = jnp.sum((move_dst.reshape(nctx, blocks) == rank).astype(jnp.int32), axis=1)
    new_keys, new_values = unpack(count, at, recv, new_keys, new_values, slots)
    parts, new_keys, new_values = lax.optimization_barrier((parts, new_keys, new_values))
    parts = parts.reshape(chips, nhead, each + 2, head_dim)
    notes = parts[:, :, each, : 3 * each].reshape(chips, nhead, 3, each).astype(jnp.float32)
    top = jnp.max(notes[:, :, 0], axis=0)
    factor = jnp.exp2((notes[:, :, 0] - top) * log_scale)
    denom = jnp.sum(factor * (notes[:, :, 1] + notes[:, :, 2]), axis=0)
    total = jnp.sum(parts[:, :, :each].astype(jnp.float32) * factor[..., None], axis=0)
    attn = (total / denom[..., None]).astype(jnp.bfloat16)
    share = own // nhead
    line = attn.reshape(nhead, share, heads, head_dim).swapaxes(0, 1).reshape(-1, head_dim)
    same = everywhere(line, "ctx", sides)
    other = across(same, "ctx")

    def project(x):
        x = x.reshape(chips * share, nhead * heads * head_dim)
        y = jnp.dot(x, weights, preferred_element_type=jnp.float32).astype(jnp.bfloat16)
        return y.reshape(chips, share, -1)

    mixed = in_order(odd, project(same), project(other)).reshape(nctx * share, -1)
    shape = (blocks + slots, width, kv_local, head_dim)
    return (mixed, new_keys.reshape(shape), new_values.reshape(shape))


def solution(mesh):
    cache = P("ctx", None, "head", None)
    in_specs = (
        P("ctx", "head"), P("ctx", "head"), P("ctx", "head"), cache, cache, P("head", "ctx"),
        P(), P(), P(), P(), P(),
    )
    out_specs = (P("head", "ctx"), cache, cache)
    return jax.shard_map(shards, mesh=mesh, in_specs=in_specs, out_specs=out_specs, check_vma=False)
```

```python
import functools
import math

import jax
import jax.numpy as jnp
from jax import lax
from jax.experimental import pallas as pl
from jax.experimental.pallas import tpu as pltpu
from jax.sharding import PartitionSpec as P

CAP = 2
STEP = 4
SHIFT = 8
LOW = -1e30


def pack_kernel(rank_ref, dst_ref, at_ref, k_ref, v_ref, send_ref, used, sems):
    blocks = k_ref.shape[0]
    base = rank_ref[0] * blocks

    def clear(d, carry):
        used[d] = 0
        return carry

    lax.fori_loop(0, used.shape[0], clear, 0)

    def copies(b, dst, place):
        return (
            pltpu.make_async_copy(k_ref.at[b], send_ref.at[(dst * CAP + place) * 2], sems.at[b, 0]),
            pltpu.make_async_copy(v_ref.at[b], send_ref.at[(dst * CAP + place) * 2 + 1], sems.at[b, 1]),
        )

    def start(b, carry):
        dst = dst_ref[base + b]

        @pl.when(dst >= 0)
        def _():
            place = jnp.minimum(used[dst], CAP - 1)
            used[dst] = place + 1
            for c in copies(b, at_ref[dst], place):
                c.start()

        return carry

    lax.fori_loop(0, blocks, start, 0)

    def finish(b, carry):
        @pl.when(dst_ref[base + b] >= 0)
        def _():
            for c in copies(b, 0, 0):
                c.wait()

        return carry

    lax.fori_loop(0, blocks, finish, 0)


def pack(rank, move_dst, at, keys, values, nctx):
    blocks, rows, lanes = keys.shape
    return pl.pallas_call(
        pack_kernel,
        out_shape=jax.ShapeDtypeStruct((nctx * CAP * 2, rows, lanes), keys.dtype),
        grid_spec=pltpu.PrefetchScalarGridSpec(
            num_scalar_prefetch=3,
            grid=(1,),
            in_specs=[pl.BlockSpec((blocks, rows, lanes), lambda i, *_: (0, 0, 0))] * 2,
            out_specs=pl.BlockSpec(memory_space=pltpu.HBM),
            scratch_shapes=[
                pltpu.SMEM((nctx,), jnp.int32),
                pltpu.SemaphoreType.DMA((blocks, 2)),
            ],
        ),
        compiler_params=pltpu.CompilerParams(vmem_limit_bytes=58 * 2**20),
        cost_estimate=pl.CostEstimate(
            flops=0, bytes_accessed=4 * blocks * rows * lanes * 2, transcendentals=0
        ),
        name="pack",
    )(rank, move_dst, at, keys, values)


def unpack_kernel(slots, count_ref, at_ref, recv_ref, _k, _v, k_out, v_out, stage, loads, stores):
    nctx = count_ref.shape[0]
    first = k_out.shape[0] - slots
    outs = (k_out, v_out)

    def load(row, place, slot, i):
        return pltpu.make_async_copy(
            recv_ref.at[(row * CAP + place) * 2 + i], stage.at[slot, i], loads.at[slot, i]
        )

    def store(slot, i):
        return pltpu.make_async_copy(stage.at[slot, i], outs[i].at[first + slot], stores.at[slot, i])

    def source(s, slot):
        count = count_ref[s]
        for place in range(CAP):

            @pl.when((count > place) & (slot + place < slots))
            def _():
                for i in range(2):
                    load(at_ref[s], place, slot + place, i).start()

        return slot + count

    filled = jnp.minimum(lax.fori_loop(0, nctx, source, 0), slots)

    def blank(slot, carry):
        stage[slot] = jnp.zeros(stage.shape[1:], stage.dtype)
        for i in range(2):
            store(slot, i).start()
        return carry

    lax.fori_loop(filled, slots, blank, 0)

    def passed(slot, carry):
        for i in range(2):
            load(0, 0, slot, i).wait()
            store(slot, i).start()
        return carry

    lax.fori_loop(0, filled, passed, 0)

    def finish(slot, carry):
        for i in range(2):
            store(slot, i).wait()
        return carry

    lax.fori_loop(0, slots, finish, 0)


def unpack(count, at, recv, keys, values, slots):
    rows, lanes = keys.shape[1:]
    shape = jax.ShapeDtypeStruct(keys.shape, keys.dtype)
    return pl.pallas_call(
        functools.partial(unpack_kernel, slots),
        out_shape=(shape, shape),
        grid_spec=pltpu.PrefetchScalarGridSpec(
            num_scalar_prefetch=2,
            grid=(1,),
            in_specs=[pl.BlockSpec(memory_space=pl.ANY)] + [pl.BlockSpec(memory_space=pltpu.HBM)] * 2,
            out_specs=[pl.BlockSpec(memory_space=pltpu.HBM)] * 2,
            scratch_shapes=[
                pltpu.VMEM((slots, 2, rows, lanes), keys.dtype),
                pltpu.SemaphoreType.DMA((slots, 2)),
                pltpu.SemaphoreType.DMA((slots, 2)),
            ],
        ),
        input_output_aliases={3: 0, 4: 1},
        cost_estimate=pl.CostEstimate(
            flops=0, bytes_accessed=8 * slots * rows * lanes, transcendentals=0
        ),
        name="unpack",
    )(count, at, recv, keys, values)


def attend(q, keys, values, column, limit, top, total, numer, r, log_scale):
    scores = lax.dot_general(q, keys, (((1,), (1,)), ((), ())), preferred_element_type=jnp.float32)
    scores = jnp.where(column < limit, scores, LOW)
    best = jnp.max(scores, axis=1, keepdims=True)
    best = best.astype(jnp.bfloat16).astype(jnp.float32)
    old = top[r]
    new = jnp.maximum(old, best)
    probs = jnp.exp2((scores - new[:, :1]) * log_scale)
    shrink = jnp.exp2((old - new) * log_scale)
    top[r] = new
    lanes = numer.shape[2]
    width = probs.shape[1]
    if width > lanes:
        part = probs[:, :lanes]
        for first in range(lanes, width, lanes):
            part = part + probs[:, first : first + lanes]
    else:
        part = jnp.concatenate(
            [probs, jnp.zeros((probs.shape[0], lanes - width), jnp.float32)], axis=1
        )
    total[r] = total[r] * shrink + part
    high = probs.astype(jnp.bfloat16)
    rest = (probs - high.astype(jnp.float32)).astype(jnp.bfloat16)
    numer[r] = (
        numer[r] * shrink
        + jnp.dot(high, values, preferred_element_type=jnp.float32)
        + jnp.dot(rest, values, preferred_element_type=jnp.float32)
    )


def attention_kernel(
    kv_local, group, log_scale,
    rank_ref, req_ref, idx_ref, dst_ref, len_ref,
    q_ref, dk_ref, dv_ref, offs_ref, k_ref, v_ref,
    numer_ref, stats_ref, k_out, v_out,
    top, total, numer, column,
):
    step = pl.program_id(0)
    requests, rows, lanes = numer.shape
    width = k_ref.shape[1] // kv_local
    blocks = pl.num_programs(0) * STEP
    rank = rank_ref[0]
    base = rank * blocks + step * STEP

    @pl.when(step == 0)
    def _():
        top[...] = jnp.full(top.shape, LOW, jnp.float32)
        total[...] = jnp.zeros(total.shape, jnp.float32)
        numer[...] = jnp.zeros(numer.shape, jnp.float32)
        line = lax.broadcasted_iota(jnp.int32, column.shape, 1)
        row = lax.broadcasted_iota(jnp.int32, column.shape, 0)
        own = row % (kv_local * group) // group
        column[...] = jnp.where(line % kv_local == own, line // kv_local, 1 << 20)

        @pl.when((rank & 3) < 3)
        def _():
            drafts = dk_ref.shape[0]
            mine = 3 * (rank >> 2) + (rank & 3)
            spot = column[:, :drafts]
            spot = jnp.where(spot >= offs_ref[...], spot, 1 << 20)
            token = lax.broadcasted_iota(jnp.int32, spot.shape, 0) // (kv_local * group)
            attend(q_ref[mine], dk_ref[...], dv_ref[...], spot, token + 1,
                   top, total, numer, mine, log_scale)

    for g in range(STEP):
        slot = base + g
        stays = dst_ref[slot] < 0

        @pl.when(stays)
        def _():
            k_out[g] = k_ref[g]
            v_out[g] = v_ref[g]

        @pl.when(jnp.logical_not(stays))
        def _():
            k_out[g] = jnp.zeros(k_out.shape[1:], k_out.dtype)
            v_out[g] = jnp.zeros(v_out.shape[1:], v_out.dtype)

        idx = idx_ref[slot]

        @pl.when(idx >= 0)
        def _():
            r = req_ref[slot]
            limit = jnp.minimum(len_ref[r] - idx * width, width)
            attend(q_ref[r], k_ref[g], v_ref[g], column[...], limit,
                   top, total, numer, r, log_scale)

    @pl.when(step == pl.num_programs(0) - 1)
    def _():
        ones = jnp.ones((8, lanes), jnp.float32)
        first = (lax.broadcasted_iota(jnp.int32, (8, lanes), 1) == 0).astype(jnp.float32)
        pick = lax.broadcasted_iota(jnp.int32, (8, rows), 0)
        turn = (((1,), (1,)), ((), ()))

        def close(r, carry):
            numer_ref[r] = numer[r].astype(numer_ref.dtype)
            sums = lax.dot_general(ones, total[r], turn, precision=lax.Precision.HIGHEST,
                                   preferred_element_type=jnp.float32)
            tops = lax.dot_general(first, top[r], turn, precision=lax.Precision.HIGHEST,
                                   preferred_element_type=jnp.float32)
            stats_ref[r] = jnp.where(pick == 0, tops, sums)
            return carry

        lax.fori_loop(0, requests, close, 0)


def attention(rank, block_req, block_idx, move_dst, lengths, q, dk, dv, offs, keys, values,
              slots, kv_local, group, log_scale):
    blocks, width, lanes = keys.shape
    requests, rows, _ = q.shape
    whole = lambda shape: pl.BlockSpec(shape, lambda i, *_: (0,) * len(shape))
    part = pl.BlockSpec((STEP, width, lanes), lambda i, *_: (i, 0, 0))
    cache = jax.ShapeDtypeStruct((blocks + slots, width, lanes), keys.dtype)
    return pl.pallas_call(
        functools.partial(attention_kernel, kv_local, group, log_scale),
        out_shape=(
            jax.ShapeDtypeStruct((requests, rows, lanes), jnp.float32),
            jax.ShapeDtypeStruct((requests, 8, rows), jnp.float32),
            cache,
            cache,
        ),
        grid_spec=pltpu.PrefetchScalarGridSpec(
            num_scalar_prefetch=5,
            grid=(blocks // STEP,),
            in_specs=[whole(q.shape), whole(dk.shape), whole(dv.shape), whole(offs.shape), part, part],
            out_specs=[whole((requests, rows, lanes)), whole((requests, 8, rows)), part, part],
            scratch_shapes=[
                pltpu.VMEM((requests, rows, lanes), jnp.float32),
                pltpu.VMEM((requests, rows, lanes), jnp.float32),
                pltpu.VMEM((requests, rows, lanes), jnp.float32),
                pltpu.VMEM((rows, width), jnp.int32),
            ],
        ),
        compiler_params=pltpu.CompilerParams(vmem_limit_bytes=40 * 2**20),
        cost_estimate=pl.CostEstimate(
            flops=4 * blocks * rows * width * lanes,
            bytes_accessed=8 * blocks * width * lanes,
            transcendentals=blocks * rows * width,
        ),
        name="attention",
    )(rank, block_req, block_idx, move_dst, lengths, q, dk, dv, offs, keys, values)


def settle_kernel(x_ref, out_ref):
    out_ref[...] = x_ref[...]


def settle(x):
    return pl.pallas_call(
        settle_kernel, out_shape=jax.ShapeDtypeStruct(x.shape, x.dtype), name="settle"
    )(x)


def exchange(x, axis, groups=None):
    return lax.all_to_all(
        x, axis, split_axis=0, concat_axis=0, tiled=True, axis_index_groups=groups
    )


def everywhere(x, axis, groups):
    return exchange(jnp.broadcast_to(x[None], (len(groups[0]), *x.shape)), axis, groups)


def around(x, axis):
    n = lax.axis_size(axis)
    here = lax.axis_index(axis)
    turns = [x] + [lax.ppermute(x, axis, [(i, (i + d) % n) for i in range(n)]) for d in range(1, n)]
    stack = jnp.stack(turns)
    return jnp.stack(
        [lax.dynamic_index_in_dim(stack, (here - i) & (n - 1), keepdims=False) for i in range(n)]
    )


def rotate(x, by):
    return jnp.concatenate([x[by:], x[:by]], axis=0)


def in_order(odd, same, other):
    even_rows, odd_rows = jnp.where(odd, other, same), jnp.where(odd, same, other)
    return jnp.stack([even_rows, rotate(odd_rows, -SHIFT)], axis=1)


def across(x, axis):
    return lax.ppermute(x, axis, [(i, i ^ 1) for i in range(lax.axis_size(axis))])


def shards(
    queries, draft_keys, draft_values, cache_keys, cache_values, w_out,
    lengths, block_req, block_idx, move_dst, draft_offs,
):
    blocks, width, kv_local, head_dim = cache_keys.shape
    nctx = lax.axis_size("ctx")
    rank = lax.axis_index("ctx").astype(jnp.int32)
    requests, drafts = draft_offs.shape
    own = queries.shape[0]
    heads = queries.shape[1] // head_dim
    group = heads // kv_local
    tokens = requests * drafts
    slots = nctx
    log_scale = math.log2(math.e) / math.sqrt(head_dim)
    me = rank.reshape(1)

    keys = cache_keys.reshape(blocks, width * kv_local, head_dim)
    values = cache_values.reshape(blocks, width * kv_local, head_dim)

    mine = queries.reshape(-1, head_dim)
    pair = jnp.concatenate([draft_keys, draft_values], axis=1)
    after = lax.ppermute(pair, "ctx", [(i, (i - 1) % nctx) for i in range(nctx)])
    chips = nctx // 2
    odd = (rank & 1) == 1
    rings = [[(i + side * SHIFT) % chips for i in range(chips)] for side in range(2)]
    sides = [[2 * i + side for i in rings[side]] for side in range(2)]
    order = [(d + x) % 4 * 8 + x * 2 + c for d in range(4) for x in range(4) for c in range(2)]
    at = jnp.asarray([order.index(i) for i in range(nctx)], jnp.int32)
    send = pack(me, move_dst, at, keys, values, nctx)
    same = everywhere(mine, "ctx", sides)
    same, send, after = lax.optimization_barrier((same, send, after))
    recv = exchange(send, "ctx", [order])
    other = across(same, "ctx")
    shared = in_order(odd, same, other)
    q = shared.reshape(requests, drafts * heads, head_dim)
    span = jnp.concatenate([pair, after], axis=0)
    span = lax.dynamic_slice_in_dim(span, (rank & 3) * (drafts - own), drafts)
    dk, dv = (
        x.reshape(drafts * kv_local, head_dim)
        for x in (span[:, : kv_local * head_dim], span[:, kv_local * head_dim :])
    )
    nhead = lax.axis_size("head")
    weights = around(w_out, "head").reshape(nhead * heads * head_dim, -1)

    my_req = jnp.minimum(3 * (rank >> 2) + (rank & 3), requests - 1)
    my_offs = lax.dynamic_slice_in_dim(draft_offs, my_req, 1)[0]
    offs = jnp.repeat(my_offs, heads)[:, None]
    numer, stats, new_keys, new_values = attention(
        me, block_req, block_idx, move_dst, lengths, q, dk, dv, offs, keys, values,
        slots, kv_local, group, log_scale,
    )
    each = own * heads // nhead

    def by_target(x):
        lanes = x.shape[-1]
        x = x.reshape(nhead, chips, 2, each, lanes)
        x = jnp.transpose(x, (2, 1, 0, 3, 4)).reshape(2, chips * nhead, each, lanes)
        even_rows, odd_rows = x[0], rotate(x[1], SHIFT * nhead)
        return jnp.where(odd, odd_rows, even_rows), jnp.where(odd, even_rows, odd_rows)

    kept, given = by_target(numer)
    kept_notes, given_notes = by_target(jnp.swapaxes(stats[:, :2], 1, 2))
    kept_notes, given_notes = kept_notes.swapaxes(1, 2), given_notes.swapaxes(1, 2)
    taken, taken_notes = across(given, "ctx"), across(given_notes, "ctx")
    pair_top = jnp.maximum(kept_notes[:, 0], taken_notes[:, 0])
    fa = jnp.exp2((kept_notes[:, 0] - pair_top) * log_scale)
    fb = jnp.exp2((taken_notes[:, 0] - pair_top) * log_scale)
    pair = (kept * fa[:, :, None] + taken * fb[:, :, None]).astype(jnp.bfloat16)
    sums = kept_notes[:, 1] * fa + taken_notes[:, 1] * fb
    high = sums.astype(jnp.bfloat16)
    rest = (sums - high.astype(jnp.float32)).astype(jnp.bfloat16)
    notes = jnp.concatenate([pair_top.astype(jnp.bfloat16), high, rest], axis=1)[:, None]
    notes = jnp.pad(notes, ((0, 0), (0, 1), (0, head_dim - 3 * each)))
    packet = jnp.concatenate([pair, notes], axis=1)
    packet = settle(packet)
    packet, recv, weights = lax.optimization_barrier((packet, recv, weights))
    groups = [
        [(2 * i + side) * nhead + h for i in rings[side] for h in range(nhead)]
        for side in range(2)
    ]
    parts = exchange(packet, ("ctx", "head"), groups)
    count = jnp.sum((move_dst.reshape(nctx, blocks) == rank).astype(jnp.int32), axis=1)
    new_keys, new_values = unpack(count, at, recv, new_keys, new_values, slots)
    parts, new_keys, new_values = lax.optimization_barrier((parts, new_keys, new_values))
    parts = parts.reshape(chips, nhead, each + 2, head_dim)
    notes = parts[:, :, each, : 3 * each].reshape(chips, nhead, 3, each).astype(jnp.float32)
    top = jnp.max(notes[:, :, 0], axis=0)
    factor = jnp.exp2((notes[:, :, 0] - top) * log_scale)
    denom = jnp.sum(factor * (notes[:, :, 1] + notes[:, :, 2]), axis=0)
    total = jnp.sum(parts[:, :, :each].astype(jnp.float32) * factor[..., None], axis=0)
    attn = (total / denom[..., None]).astype(jnp.bfloat16)
    share = own // nhead
    line = attn.reshape(nhead, share, heads, head_dim).swapaxes(0, 1).reshape(-1, head_dim)
    same = everywhere(line, "ctx", sides)
    other = across(same, "ctx")

    def project(x):
        x = x.reshape(chips * share, nhead * heads * head_dim)
        y = jnp.dot(x, weights, preferred_element_type=jnp.float32).astype(jnp.bfloat16)
        return y.reshape(chips, share, -1)

    mixed = in_order(odd, project(same), project(other)).reshape(nctx * share, -1)
    shape = (blocks + slots, width, kv_local, head_dim)
    return (mixed, new_keys.reshape(shape), new_values.reshape(shape))


def solution(mesh):
    cache = P("ctx", None, "head", None)
    in_specs = (
        P("ctx", "head"), P("ctx", "head"), P("ctx", "head"), cache, cache, P("head", "ctx"),
        P(), P(), P(), P(), P(),
    )
    out_specs = (P("head", "ctx"), cache, cache)
    return jax.shard_map(shards, mesh=mesh, in_specs=in_specs, out_specs=out_specs, check_vma=False)
```
